128 devices in a mesh: section: 2 (over x_lo), dp: 8 (over x_hi, y), tensor: 8 (over z, core).
Axes of the slice: x: 4 (x_hi: 2, x_lo: 2; x = x_hi * 2 + x_lo), y: 4, z: 4, core: 2. Of those that a mesh axis runs over, the one named last changes fastest.
Arguments:
- tokens: bfloat16 [2048, 8192], P('dp', ('section', 'tensor')), may hold values from -6 to 6
- segment_ids: int32 [8, 256], P('dp'), may hold values from 0 to 3, never falling along the last dimension, each value on 1 to 128 neighbouring positions
- gain_attn: float32 [8192], replicated, may hold values from 0.1 to 1.9
- w_query: bfloat16 [8192, 4096], P(None, ('section', 'tensor')), may hold values from -0.06629126 to 0.06629126
- w_key: bfloat16 [8192, 4096], P(None, ('section', 'tensor')), may hold values from -0.06629126 to 0.06629126
- w_value: bfloat16 [8192, 4096], P(None, ('section', 'tensor')), may hold values from -0.0625 to 0.0625
- w_output: bfloat16 [4096, 8192], P(('section', 'tensor')), may hold values from -0.09375 to 0.09375
- gain_ffn: float32 [8192], replicated, may hold values from 0.1 to 1.9
- w_up: bfloat16 [8192, 16384], P(('section', 'tensor'), 'dp'), may hold values from -0.0625 to 0.0625
- w_down: bfloat16 [16384, 8192], P('dp', ('section', 'tensor')), may hold values from -0.046875 to 0.046875
Outputs:
- layer_out: bfloat16 [2048, 8192], P('dp', ('section', 'tensor'))
The draws below stay inside these ranges and needn't reach their ends.
Inputs may be any that keep to these rules, and one draw needn't show every extreme that they name: `segment_ids`: segment numbers never fall along a replica's tokens; each segment holds 1 to 128 tokens.
All inputs are finite; a program needn't handle non-finite values.
Results may differ from the reference program's by a relative error of at most 0.023.
Values may be sent and summed in bfloat16 or wider, within the bound.
A program may use at most 128 MiB of HBM per device.

```python
import math
import jax
import jax.numpy as jnp
import numpy as np
from jax import lax

D = 8192
HEADS = 32
HD = 128
FF = 16384
TOK = 256
TOKENS = 2048
N_SECTION = 2
N_DP = 8
N_TENSOR = 8


def draw_tokens(key, part):
    key = jax.random.fold_in(key, 3)
    return jnp.clip(jax.random.normal(key, (TOKENS, D), jnp.float32), -6.0, 6.0).astype(jnp.bfloat16)


def draw_w_query(key, part):
    key = jax.random.fold_in(key, 5)
    spread = D ** (-0.5)
    return (jnp.clip(jax.random.normal(key, (D, HEADS * HD), jnp.float32), -6.0, 6.0) * spread).astype(jnp.bfloat16)


def draw_w_key(key, part):
    key = jax.random.fold_in(key, 7)
    spread = D ** (-0.5)
    return (jnp.clip(jax.random.normal(key, (D, HEADS * HD), jnp.float32), -6.0, 6.0) * spread).astype(jnp.bfloat16)


def shard_levels(rng, extent, cuts, least, top_value):
    factor_of, own = 1.0, jax.random.fold_in(rng, 6)
    for dim, shards_of in cuts:
        heights = jnp.exp(jax.random.uniform(jax.random.fold_in(own, dim), (shards_of,), jnp.float32, least / len(cuts), top_value / len(cuts)))
        factor_of = factor_of * jnp.repeat(heights, extent[dim] // shards_of).reshape([-1 if axis == dim else 1 for axis in range(len(extent))])
    return factor_of


def profile(amount, total, reach, lean):
    portions = [(1 << 20) // math.isqrt(rank ** lean) + 1 for rank in range(2, amount + 1)]
    surplus, holding = total - reach - (amount - 1), [1] * (amount - 1)
    while surplus > 0:
        candidates = [i for i in range(amount - 1) if holding[i] < reach]
        mass, remaining = sum([portions[i] for i in candidates]), surplus
        for i in candidates:
            more = min(reach - holding[i], max(1, remaining * portions[i] // mass), surplus)
            holding[i] = holding[i] + more
            surplus = surplus - more
    return np.array([reach] + holding)


def uneven_parts(own_key, number_of, total, bound, slope):
    if number_of == 2:
        one = jax.random.randint(own_key, (), max(1, total - bound), min(bound, total - 1) + 1)
        return jnp.stack([one, total - one])
    sizes = jnp.asarray(profile(number_of, total, bound, slope), jnp.int32)
    couples = (number_of - 1) // 2
    source_of, sink = sizes[1:1 + 2 * couples:2], sizes[2:2 + 2 * couples:2]
    slack = jnp.minimum(source_of - 1, bound - sink)
    passed = jax.random.randint(jax.random.fold_in(own_key, 1), (couples,), 0, 1 << 20) % (slack + 1)
    sizes = sizes.at[1:1 + 2 * couples:2].set(source_of - passed).at[2:2 + 2 * couples:2].set(sink + passed)
    return sizes[jax.random.permutation(jax.random.fold_in(own_key, 2), number_of)]


def noise(stream_key, dims, scale, limit, shards=(), dtype=jnp.bfloat16):
    loudness = shard_levels(stream_key, dims, shards, -0.22, 0.18) if shards else 1.0
    result = jax.random.normal(stream_key, dims, jnp.float32) * scale * loudness
    return jnp.minimum(jnp.maximum(result, -limit), limit).astype(dtype)


def setup_inputs(seed: int = 0) -> dict:
    keys = jax.random.split(jax.random.key(seed), 11)
    return {
        "tokens": draw_tokens(jax.random.fold_in(keys[10], 71), 0),
        "segment_ids": jax.vmap(lambda own: jnp.searchsorted(jnp.cumsum(uneven_parts(own, 4, TOK, TOK // 2, 2)), jnp.arange(TOK), side="right"))(jax.random.split(keys[1], N_DP)).reshape((N_DP, TOK)).astype(jnp.int32),
        "gain_attn": jnp.clip(1.0 + 0.18 * jax.random.normal(keys[2], (D,), jnp.float32), 0.1, 1.9),
        "w_query": draw_w_query(jax.random.fold_in(keys[10], 71), 0),
        "w_key": draw_w_key(jax.random.fold_in(keys[10], 71), 0),
        "w_value": noise(keys[5], (D, HEADS * HD), D ** -0.5, 0.0625, ((1, 16),)),
        "w_output": noise(keys[6], (HEADS * HD, D), (HEADS * HD) ** -0.5, 0.09375, ((0, 16),)),
        "gain_ffn": jnp.clip(1.0 + 0.18 * jax.random.normal(keys[7], (D,), jnp.float32), 0.1, 1.9),
        "w_up": noise(keys[8], (D, FF), D ** -0.5, 0.0625, ((0, 16), (1, 8))),
        "w_down": noise(keys[9], (FF, D), FF ** -0.5, 0.046875, ((0, 8), (1, 16))),
    }


def layer_norm(values, gain):
    mean = lax.optimization_barrier(jnp.mean(values, axis=-1, keepdims=True))
    second = lax.optimization_barrier(jnp.mean(values * values, axis=-1, keepdims=True))
    return (values - mean) * lax.rsqrt(second - mean * mean + 1e-05) * gain

def blocked_product(left, right, count):
    size = left.shape[1] // count
    start_acc = jnp.zeros((left.shape[0], right.shape[1]), jnp.float32)

    def step(index, acc):
        piece_left = lax.dynamic_slice_in_dim(left, index * size, size, 1)
        piece_right = lax.dynamic_slice_in_dim(right, index * size, size, 0)
        term = jnp.dot(piece_left, piece_right, preferred_element_type=jnp.float32).astype(jnp.bfloat16)
        term = lax.optimization_barrier(term)
        return acc + term.astype(jnp.float32)
    return lax.fori_loop(0, count, step, start_acc)

def reference(tokens, segment_ids, gain_attn, w_query, w_key, w_value, w_output, gain_ffn, w_up, w_down):
    normed = layer_norm(tokens.astype(jnp.float32), gain_attn).astype(jnp.bfloat16)
    query = jnp.dot(normed, w_query, preferred_element_type=jnp.float32).astype(jnp.bfloat16)
    key = jnp.dot(normed, w_key, preferred_element_type=jnp.float32).astype(jnp.bfloat16)
    value = jnp.dot(normed, w_value, preferred_element_type=jnp.float32).astype(jnp.bfloat16)
    shape = (N_DP, TOK, HEADS, HD)
    query = query.reshape(shape).astype(jnp.float32)
    key = key.reshape(shape).astype(jnp.float32)
    value = value.reshape(shape).astype(jnp.float32)
    scores = jnp.einsum('bqhd,bkhd->bhqk', query, key) * HD ** (-0.5)
    position = jnp.arange(TOK)
    causal = position[:, None] >= position[None, :]
    same = segment_ids[:, :, None] == segment_ids[:, None, :]
    keep = jnp.logical_and(causal[None], same)[:, None]
    scores = jnp.where(keep, scores, -1e+30)
    top = lax.optimization_barrier(jnp.max(scores, axis=-1, keepdims=True))
    expo = jnp.exp(scores - top)
    probs = (expo / lax.optimization_barrier(jnp.sum(expo, axis=-1, keepdims=True))).astype(jnp.bfloat16)
    context = jnp.einsum('bhqk,bkhd->bqhd', probs.astype(jnp.float32), value)
    context = context.astype(jnp.bfloat16).reshape(N_DP * TOK, HEADS * HD)
    attn = jnp.dot(context, w_output, preferred_element_type=jnp.float32)
    resid_mid = (tokens.astype(jnp.float32) + attn).astype(jnp.bfloat16)
    normed_ffn = layer_norm(resid_mid.astype(jnp.float32), gain_ffn).astype(jnp.bfloat16)
    pre_act = blocked_product(normed_ffn, w_up, N_SECTION * N_TENSOR)
    activated = jax.nn.gelu(pre_act, approximate=True).astype(jnp.bfloat16)
    ffn_out = blocked_product(activated, w_down, N_DP)
    return (resid_mid.astype(jnp.float32) + ffn_out).astype(jnp.bfloat16)
```

```python
import jax
import jax.numpy as jnp
from jax import lax
from jax.experimental import pallas as pl
from jax.experimental.pallas import tpu as pltpu
from jax.sharding import PartitionSpec as P

MESH = pl.DeviceIdType.MESH
HD = 128
F32 = jnp.float32
BF16 = jnp.bfloat16
N_G = 16
N_DP = 8


def remote(src, dst, send_sem, recv_sem, device):
    return pltpu.make_async_remote_copy(
        src_ref=src,
        dst_ref=dst,
        send_sem=send_sem,
        recv_sem=recv_sem,
        device_id=device,
        device_id_type=MESH,
    )


def rows_to_columns(row, width):
    column = jnp.transpose(jnp.broadcast_to(row, (128, row.shape[1])))
    return jnp.concatenate([column] * (width // 128), axis=1)


def partial_stats(values):
    ones = jnp.ones((8, values.shape[1]), BF16)
    dims = (((1,), (1,)), ((), ()))
    wide = values.astype(F32)
    square = wide * wide
    high = square.astype(BF16)
    low = (square - high.astype(F32)).astype(BF16)
    total = lax.dot_general(ones, values, dims, preferred_element_type=F32)
    second = lax.dot_general(ones, high, dims, preferred_element_type=F32)
    second += lax.dot_general(ones, low, dims, preferred_element_type=F32)
    return jnp.where(lax.broadcasted_iota(jnp.int32, total.shape, 0) == 0, total, second)


def attention_kernel(
    tok_ref, seg_ref, gain_a_ref, gain_f_ref, wq_hbm, wk_hbm, wv_hbm, wo_hbm,
    resid_ref, normed_ref,
    wq, wk, wv, wo, tok, acc, part, sib, land, stat_own, stats, mu, scale,
    w_sem, ag_send, ag_recv, sib_send, sib_recv, rs_send, rs_recv, st_send, st_recv,
):
    a = lax.axis_index("section")
    t = lax.axis_index("tensor")
    z, c = t // 2, t % 2
    oa, oc = 1 - a, 1 - c
    zp, zm, z2 = (z + 1) % 4, (z + 3) % 4, (z + 2) % 4
    me = a * 8 + t

    def dev(a_, z_, c_):
        return {"section": a_, "tensor": z_ * 2 + c_}

    def slot(a_, z_, c_):
        return a_ * 8 + z_ * 2 + c_

    def peer(r):
        i = (me + r) % N_G
        return i, {"section": i // 8, "tensor": i % 8}

    barrier = pltpu.get_barrier_semaphore()

    @pl.loop(1, N_G)
    def _(r):
        pl.semaphore_signal(barrier, inc=1, device_id=peer(r)[1], device_id_type=MESH)

    loads = [
        pltpu.make_async_copy(h, v, w_sem.at[n])
        for n, (h, v) in enumerate(((wq_hbm, wq), (wk_hbm, wk), (wv_hbm, wv), (wo_hbm, wo)))
    ]
    for load in loads:
        load.start()
    stat_own[0] = partial_stats(tok_ref[...])
    stats[0, me] = stat_own[0]
    tok[me] = tok_ref[...]
    pl.semaphore_wait(barrier, N_G - 1)

    def stat_copy(n, r):
        i, device = peer(r)
        return remote(stat_own.at[n], stats.at[n, me], st_send.at[n, r], st_recv.at[n, me], device)

    def stat_wait(n, r):
        i, device = peer(r)
        remote(stat_own.at[n], stats.at[n, i], st_send.at[n, r], st_recv.at[n, i], device).wait_recv()

    def exchange(n):
        @pl.loop(1, N_G)
        def _(r):
            stat_copy(n, r).start()

    def norm_of(n, width):
        @pl.loop(1, N_G)
        def _(r):
            stat_wait(n, r)

        total = jnp.sum(stats[n], axis=0)
        mean = total[0:1] / 8192.0
        second = total[1:2] / 8192.0
        inverse = lax.rsqrt(second - mean * mean + 1e-05)
        mu[...] = rows_to_columns(mean, width)
        scale[...] = rows_to_columns(inverse, width)

    def ag(n, s, device):
        return remote(tok.at[s], tok.at[s], ag_send.at[n], ag_recv.at[s], device)

    own = slot(a, z, c)
    exchange(0)
    sends = []

    def go(copy):
        copy.start()
        sends.append(copy)

    def arrived(s):
        ag(0, s, dev(a, zp, c)).wait_recv()

    def to_sib(n, s):
        go(ag(n, s, dev(a, z, oc)))

    go(ag(0, own, dev(oa, z, c)))
    go(ag(1, own, dev(a, zp, c)))
    go(ag(2, own, dev(a, zm, c)))
    to_sib(3, own)
    go(ag(4, own, dev(a, z2, c)))
    norm_of(0, 512)
    acc[...] = jnp.zeros_like(acc)

    def project(s):
        x = (tok[s].astype(F32) - mu[...]) * scale[...] * gain_a_ref[s]
        x = x.astype(BF16)
        at = pl.ds(pl.multiple_of(s * 512, 512), 512)
        for n, w in enumerate((wq, wk, wv)):
            acc[:, n * 256 : (n + 1) * 256] += jnp.dot(x, w[at, :], preferred_element_type=F32)

    for load in loads[:3]:
        load.wait()
    project(own)
    s_x, s_zp, s_zm, s_z2 = slot(oa, z, c), slot(a, zp, c), slot(a, zm, c), slot(a, z2, c)
    s_xzp, s_xzm, s_xz2 = slot(oa, zp, c), slot(oa, zm, c), slot(oa, z2, c)
    arrived(slot(a, z, oc))
    project(slot(a, z, oc))
    arrived(s_x)
    go(ag(5, s_x, dev(a, zp, c)))
    go(ag(6, s_x, dev(a, zm, c)))
    to_sib(7, s_x)
    project(s_x)
    arrived(s_zp)
    to_sib(8, s_zp)
    project(s_zp)
    arrived(s_zm)
    to_sib(9, s_zm)
    project(s_zm)
    arrived(slot(oa, z, oc))
    project(slot(oa, z, oc))
    arrived(slot(a, zp, oc))
    project(slot(a, zp, oc))
    arrived(slot(a, zm, oc))
    project(slot(a, zm, oc))
    arrived(s_z2)
    go(ag(10, s_z2, dev(oa, z, c)))
    to_sib(11, s_z2)
    project(s_z2)
    arrived(slot(a, z2, oc))
    project(slot(a, z2, oc))
    for n, s in ((12, s_xzp), (13, s_xzm), (14, s_xz2)):
        arrived(s)
        to_sib(n, s)
        project(s)
    for z_ in (zp, zm, z2):
        arrived(slot(oa, z_, oc))
        project(slot(oa, z_, oc))

    rows = tok_ref.shape[0]
    seg_row = seg_ref[...].astype(F32)
    seg_col = rows_to_columns(seg_row, rows)
    at_q = lax.broadcasted_iota(jnp.int32, (rows, rows), 0)
    at_k = lax.broadcasted_iota(jnp.int32, (rows, rows), 1)
    keep = jnp.logical_and(at_q >= at_k, seg_col == seg_row)
    contexts = []
    for head in range(2):
        q, k, v = (
            acc[:, n * 256 + head * HD : n * 256 + (head + 1) * HD].astype(BF16) for n in range(3)
        )
        scores = lax.dot_general(q, k, (((1,), (1,)), ((), ())), preferred_element_type=F32)
        scores = jnp.where(keep, scores * HD ** (-0.5), -1e30)
        expo = jnp.exp(scores - jnp.max(scores, axis=-1, keepdims=True))
        probs = (expo / jnp.sum(expo, axis=-1, keepdims=True)).astype(BF16)
        contexts.append(jnp.dot(probs, v, preferred_element_type=F32).astype(BF16))
    context = jnp.concatenate(contexts, axis=1)
    loads[3].wait()

    def term(s):
        at = pl.ds(pl.multiple_of(s * 512, 512), 512)
        return jnp.dot(context, wo[:, at], preferred_element_type=F32)

    order = ((oa, z2), (oa, zp), (oa, zm), (a, zp), (a, zm), (a, z2), (oa, z), (a, z))

    def sib_copy(n):
        a_, z_ = order[n]
        return remote(part.at[oc, n], sib.at[n], sib_send.at[n], sib_recv.at[n], dev(a, z, oc))

    def pair(n):
        a_, z_ = order[n]
        mine = term(slot(a_, z_, c))
        sib_copy(n).wait_recv()
        return mine + sib[n].astype(F32)

    for n, (a_, z_) in enumerate(order):
        part[oc, n] = term(slot(a_, z_, oc)).astype(BF16)
        go(sib_copy(n))

    def reduce_copy(n, device):
        return remote(part.at[c, n], land.at[n], rs_send.at[n], rs_recv.at[n], device)

    targets = (
        dev(oa, z, c), dev(a, zp, c), dev(a, zm, c), dev(a, zp, c), dev(a, zm, c),
        dev(a, z2, c), dev(oa, z, c),
    )
    for n in range(5):
        part[c, n] = pair(n).astype(BF16)
        go(reduce_copy(n, targets[n]))
    far, across, mine = pair(5), pair(6), pair(7)

    def landed(n):
        reduce_copy(n, targets[n]).wait_recv()
        return land[n].astype(F32)

    part[c, 5] = (far + landed(0)).astype(BF16)
    go(reduce_copy(5, targets[5]))
    part[c, 6] = (across + landed(1) + landed(2)).astype(BF16)
    go(reduce_copy(6, targets[6]))
    total = mine + landed(3) + landed(4) + landed(6) + landed(5)
    resid = (tok_ref[...].astype(F32) + total).astype(BF16)
    resid_ref[...] = resid
    stat_own[1] = partial_stats(resid)
    stats[1, me] = stat_own[1]
    exchange(1)
    norm_of(1, 512)
    normed = (resid.astype(F32) - mu[...]) * scale[...] * gain_f_ref[me]
    normed_ref[...] = normed.astype(BF16)

    for copy in sends:
        copy.wait_send()
    for n in range(2):

        @pl.loop(1, N_G)
        def _(r):
            stat_copy(n, r).wait_send()


def attention(tokens, segment_ids, gain_attn, gain_ffn, w_query, w_key, w_value, w_output):
    rows, share = tokens.shape
    vmem, hbm = pl.BlockSpec(memory_space=pltpu.VMEM), pl.BlockSpec(memory_space=pl.ANY)
    out = jax.ShapeDtypeStruct((rows, share), BF16)
    return pl.pallas_call(
        attention_kernel,
        out_shape=(out, out),
        in_specs=[vmem] * 4 + [hbm] * 4,
        out_specs=(vmem, vmem),
        scratch_shapes=[
            pltpu.VMEM(w_query.shape, BF16),
            pltpu.VMEM(w_query.shape, BF16),
            pltpu.VMEM(w_query.shape, BF16),
            pltpu.VMEM(w_output.shape, BF16),
            pltpu.VMEM((N_G, rows, share), BF16),
            pltpu.VMEM((rows, 768), F32),
            pltpu.VMEM((2, 8, rows, share), BF16),
            pltpu.VMEM((8, rows, share), BF16),
            pltpu.VMEM((7, rows, share), BF16),
            pltpu.VMEM((2, 8, rows), F32),
            pltpu.VMEM((2, N_G, 8, rows), F32),
            pltpu.VMEM((rows, share), F32),
            pltpu.VMEM((rows, share), F32),
            pltpu.SemaphoreType.DMA((4,)),
            pltpu.SemaphoreType.DMA((15,)),
            pltpu.SemaphoreType.DMA((N_G,)),
            pltpu.SemaphoreType.DMA((8,)),
            pltpu.SemaphoreType.DMA((8,)),
            pltpu.SemaphoreType.DMA((7,)),
            pltpu.SemaphoreType.DMA((7,)),
            pltpu.SemaphoreType.DMA((2, N_G)),
            pltpu.SemaphoreType.DMA((2, N_G)),
        ],
        compiler_params=pltpu.CompilerParams(
            collective_id=0, has_side_effects=True, vmem_limit_bytes=48 << 20
        ),
        name="attention",
    )(
        tokens, segment_ids, gain_attn.reshape(N_G, 1, share), gain_ffn.reshape(N_G, 1, share),
        w_query, w_key, w_value, w_output,
    )


SB, RX1, RZP, RZM, FZP, FZM, FZ2, FX, AZP, AZM, AZ2, AX, XZP, XZM, XZ2, AS = range(16)


def ffn_kernel(
    n_ref, r_ref, wu_hbm, wd_hbm,
    o_ref,
    wu, wd, nb, up, sb, land, act, down, fin,
    w_sem, send, recv, nb_send, nb_recv, dp_send, dp_recv,
):
    a = lax.axis_index("section")
    t = lax.axis_index("tensor")
    d = lax.axis_index("dp")
    z, c = t // 2, t % 2
    xh, y = d // 4, d % 4
    oa, oc = 1 - a, 1 - c
    zp, zm, z2 = (z + 1) % 4, (z + 3) % 4, (z + 2) % 4

    def dev(a_, z_, c_):
        return {"section": a_, "tensor": z_ * 2 + c_}

    D_X, D_ZP, D_ZM, D_Z2, D_S = dev(oa, z, c), dev(a, zp, c), dev(a, zm, c), dev(a, z2, c), dev(a, z, oc)

    def at_dp(d_):
        return {"dp": d_}

    def dp_of(k):
        dx = ((k + 1) // 4) % 2
        dy = ((k + 1) % 4 + 3 - 3 * dx) % 4
        return ((xh + dx) % 2) * 4 + (y + dy) % 4

    barrier = pltpu.get_barrier_semaphore()
    for device in (D_X, D_ZP, D_ZM, D_Z2, D_S):
        pl.semaphore_signal(barrier, inc=1, device_id=device, device_id_type=MESH)

    @pl.loop(1, N_DP)
    def _(r):
        pl.semaphore_signal(barrier, inc=1, device_id=at_dp((d + r) % N_DP), device_id_type=MESH)

    loads = [
        pltpu.make_async_copy(wu_hbm, wu, w_sem.at[0]),
        pltpu.make_async_copy(wd_hbm, wd, w_sem.at[1]),
    ]
    for load in loads:
        load.start()
    nb[d] = n_ref[...]
    pl.semaphore_wait(barrier, 5 + N_DP - 1)

    def nb_copy(n, s, device):
        return remote(nb.at[s], nb.at[s], nb_send.at[n], nb_recv.at[s], device)

    def y_of(dy):
        return xh * 4 + (y + dy) % 4

    across = (1 - xh) * 4 + y
    nb_sends = [
        nb_copy(0, d, at_dp(y_of(1))),
        nb_copy(1, d, at_dp(y_of(3))),
        nb_copy(2, d, at_dp(across)),
        nb_copy(3, d, at_dp(y_of(2))),
    ]
    nb_forwards = [nb_copy(3 + dy, across, at_dp(y_of(dy))) for dy in (1, 2, 3)]
    for copy in nb_sends:
        copy.start()

    def block(k, a_, z_):
        return up.at[k, c, a_ * 4 + z_]

    def act_block(k, a_, z_):
        return act.at[k, c, a_ * 4 + z_]

    def copy_of(kind, k):
        b = land.at[k, kind - 1] if RX1 <= kind <= FX else None
        src, dst, device = {
            SB: lambda: (up.at[k, oc], sb.at[k], D_S),
            RX1: lambda: (block(k, oa, z2), b, D_X),
            RZP: lambda: (block(k, oa, zp), b, D_ZP),
            RZM: lambda: (block(k, oa, zm), b, D_ZM),
            FZP: lambda: (block(k, a, zp), b, D_ZP),
            FZM: lambda: (block(k, a, zm), b, D_ZM),
            FZ2: lambda: (block(k, a, z2), b, D_Z2),
            FX: lambda: (block(k, oa, z), b, D_X),
            AZP: lambda: (act_block(k, a, z),) * 2 + (D_ZP,),
            AZM: lambda: (act_block(k, a, z),) * 2 + (D_ZM,),
            AZ2: lambda: (act_block(k, a, z),) * 2 + (D_Z2,),
            AX: lambda: (act_block(k, a, z),) * 2 + (D_X,),
            XZP: lambda: (act_block(k, oa, z),) * 2 + (D_ZP,),
            XZM: lambda: (act_block(k, oa, z),) * 2 + (D_ZM,),
            XZ2: lambda: (act_block(k, a, z2),) * 2 + (D_X,),
            AS: lambda: (act.at[k, c], act.at[k, c], D_S),
        }[kind]()
        return remote(src, dst, send.at[k, kind], recv.at[k, kind], device)

    def arrived(kind, k):
        if kind < AZP:
            copy_of(kind, k).wait_recv()
            return
        ref = {
            AZP: lambda: act_block(k, a, zm),
            AZM: lambda: act_block(k, a, zp),
            AZ2: lambda: act_block(k, a, z2),
            AX: lambda: act_block(k, oa, z),
            XZP: lambda: act_block(k, oa, zm),
            XZM: lambda: act_block(k, oa, zp),
            XZ2: lambda: act_block(k, oa, z2),
            AS: lambda: act.at[k, oc],
        }[kind]()
        remote(ref, ref, send.at[k, kind], recv.at[k, kind], D_X).wait_recv()

    def landed(kind, k):
        arrived(kind, k)
        return land[k, kind - 1].astype(F32)

    def up_product(k):
        s = dp_of(k)

        @pl.when(jnp.logical_and(k != 0, k != 3))
        def _():
            nb_copy(0, s, at_dp(across)).wait_recv()

        @pl.when(k == 2)
        def _():
            nb_copy(0, across, at_dp(across)).wait_recv()
            for copy in nb_forwards:
                copy.start()

        x = nb[s]
        for n in range(4):
            cols = slice(n * 512, (n + 1) * 512)
            r = jnp.dot(x, wu[:, cols], preferred_element_type=F32)
            up[k, :, :, :, cols] = r.astype(BF16).reshape(2, 8, 16, 512)
        copy_of(SB, k).start()

    def pair_sum(k):
        arrived(SB, k)
        up[k, c] = (up[k, c].astype(F32) + sb[k].astype(F32)).astype(BF16)
        for kind in (RX1, RZP, RZM, FZP, FZM):
            copy_of(kind, k).start()

    def second_sum(k):
        b = a * 4 + z2
        up[k, c, b] = (up[k, c, b].astype(F32) + landed(RX1, k)).astype(BF16)
        copy_of(FZ2, k).start()
        b = oa * 4 + z
        up[k, c, b] = (up[k, c, b].astype(F32) + landed(RZP, k) + landed(RZM, k)).astype(BF16)
        copy_of(FX, k).start()

    def activate(k):
        b = a * 4 + z
        pre = up[k, c, b].astype(F32) + landed(FZP, k) + landed(FZM, k) + landed(FZ2, k) + landed(FX, k)
        inner = 0.7978845608028654 * (pre + 0.044715 * (pre * pre * pre))
        act[k, c, b] = (0.5 * pre * (1.0 + jnp.tanh(inner))).astype(BF16)
        for kind in (AX, AZP, AZM, AZ2):
            copy_of(kind, k).start()

    def spread(k):
        arrived(AX, k)
        copy_of(XZP, k).start()
        copy_of(XZM, k).start()
        arrived(AZ2, k)
        copy_of(XZ2, k).start()

    def to_sibling(k):
        for kind in (AZP, AZM, XZP, XZM, XZ2):
            arrived(kind, k)
        copy_of(AS, k).start()

    def dp_copy(k):
        return remote(down.at[k], fin.at[d], dp_send.at[k], dp_recv.at[d], at_dp(dp_of(k)))

    def down_product(k):
        arrived(AS, k)
        x = act[k].reshape(256, 2048)
        down[k] = jnp.dot(x, wd[...], preferred_element_type=F32).astype(BF16)

        @pl.when(k > 0)
        def _():
            dp_copy(k).start()

    loads[0].wait()
    up_product(0)
    loads[1].wait()

    @pl.loop(0, N_DP + 4)
    def _(step):
        def stage(f, lag):
            k = step - lag

            @pl.when(jnp.logical_and(k >= 0, k < N_DP))
            def _():
                f(k)

        stage(pair_sum, 0)
        stage(second_sum, 1)
        stage(activate, 2)
        stage(spread, 3)
        stage(to_sibling, 4)
        stage(up_product, -1)
        stage(down_product, 4)

    total = r_ref[...].astype(F32) + down[0].astype(F32)
    for r in range(1, N_DP):
        s = (d + r) % N_DP
        remote(down.at[0], fin.at[s], dp_send.at[0], dp_recv.at[s], at_dp(across)).wait_recv()
        total += fin[s].astype(F32)
    o_ref[...] = total.astype(BF16)

    for copy in nb_sends + nb_forwards:
        copy.wait_send()

    @pl.loop(0, N_DP)
    def _(k):
        for kind in range(16):
            copy_of(kind, k).wait_send()

        @pl.when(k > 0)
        def _():
            dp_copy(k).wait_send()


def ffn(normed, resid, w_up, w_down):
    rows, share = normed.shape
    vmem, hbm = pl.BlockSpec(memory_space=pltpu.VMEM), pl.BlockSpec(memory_space=pl.ANY)
    hid = w_up.shape[1]
    return pl.pallas_call(
        ffn_kernel,
        out_shape=jax.ShapeDtypeStruct((rows, share), BF16),
        in_specs=[vmem, vmem, hbm, hbm],
        out_specs=vmem,
        scratch_shapes=[
            pltpu.VMEM(w_up.shape, BF16),
            pltpu.VMEM(w_down.shape, BF16),
            pltpu.VMEM((N_DP, rows, share), BF16),
            pltpu.VMEM((N_DP, 2, 8, 16, hid), BF16),
            pltpu.VMEM((N_DP, 8, 16, hid), BF16),
            pltpu.VMEM((N_DP, 7, 16, hid), BF16),
            pltpu.VMEM((N_DP, 2, 8, 16, hid), BF16),
            pltpu.VMEM((N_DP, rows, share), BF16),
            pltpu.VMEM((N_DP, rows, share), BF16),
            pltpu.SemaphoreType.DMA((2,)),
            pltpu.SemaphoreType.DMA((N_DP, 16)),
            pltpu.SemaphoreType.DMA((N_DP, 16)),
            pltpu.SemaphoreType.DMA((7,)),
            pltpu.SemaphoreType.DMA((N_DP,)),
            pltpu.SemaphoreType.DMA((N_DP,)),
            pltpu.SemaphoreType.DMA((N_DP,)),
        ],
        compiler_params=pltpu.CompilerParams(
            collective_id=1, has_side_effects=True, vmem_limit_bytes=52 << 20
        ),
        name="ffn",
    )(normed, resid, w_up, w_down)


def per_device(
    tokens, segment_ids, gain_attn, w_query, w_key, w_value, w_output, gain_ffn, w_up, w_down
):
    resid, normed = attention(
        tokens, segment_ids, gain_attn, gain_ffn, w_query, w_key, w_value, w_output
    )
    return ffn(normed, resid, w_up, w_down)


def solution(mesh):
    return jax.shard_map(
        per_device,
        mesh=mesh,
        in_specs=(
            P("dp", ("section", "tensor")),
            P("dp", None),
            P(),
            P(None, ("section", "tensor")),
            P(None, ("section", "tensor")),
            P(None, ("section", "tensor")),
            P(("section", "tensor"), None),
            P(),
            P(("section", "tensor"), "dp"),
            P("dp", ("section", "tensor")),
        ),
        out_specs=P("dp", ("section", "tensor")),
        check_vma=False,
    )
```

```python
import jax
import jax.numpy as jnp
from jax import lax
from jax.experimental import pallas as pl
from jax.experimental.pallas import tpu as pltpu
from jax.sharding import PartitionSpec as P

MESH = pl.DeviceIdType.MESH
HD = 128
F32 = jnp.float32
BF16 = jnp.bfloat16
N_G = 16
N_DP = 8
HALF = 128
WIDE = 512

CHUNKS = (
    (0, 0), (0, 3), (0, 1), (0, 2), (0, 7), (0, 6), (1, 3), (1, 1),
    (0, 5), (1, 7), (1, 6), (1, 5), (0, 4), (1, 2), (1, 4), (1, 0),
)
N_K = len(CHUNKS)
CHUNK_OF = {chunk: k for k, chunk in enumerate(CHUNKS)}
FORWARD_AT = (2, 7)
DIRECT_SUM = 6
DIRECT_GATHER = 11
RING = 8

(
    SB, RX1, RZP, RZM, FX, FZP1, FZM0, H0, H1, FZP0, FZM1, FZP, FZM, FZ2,
    AX, AZP, AZM, XZP, XZM, XZ2, AS, ZH0, ZH1, AZ2,
) = range(24)
KINDS = 24
L_RX1, L_RZP, L_RZM, L_FX, L_FZP, L_FZM, L_H = range(7)


def remote(src, dst, send_sem, recv_sem, device):
    return pltpu.make_async_remote_copy(
        src_ref=src,
        dst_ref=dst,
        send_sem=send_sem,
        recv_sem=recv_sem,
        device_id=device,
        device_id_type=MESH,
    )


def pick(k, values):
    result = jnp.int32(values[0])
    for i, value in enumerate(values[1:], 1):
        result = jnp.where(k == i, jnp.int32(value), result)
    return result


def rows_to_columns(row, width):
    column = jnp.transpose(jnp.broadcast_to(row, (128, row.shape[1])))
    return jnp.concatenate([column] * (width // 128), axis=1)


def partial_stats(values):
    ones = jnp.ones((8, values.shape[1]), BF16)
    dims = (((1,), (1,)), ((), ()))
    wide = values.astype(F32)
    square = wide * wide
    high = square.astype(BF16)
    low = (square - high.astype(F32)).astype(BF16)
    total = lax.dot_general(ones, values, dims, preferred_element_type=F32)
    second = lax.dot_general(ones, high, dims, preferred_element_type=F32)
    second += lax.dot_general(ones, low, dims, preferred_element_type=F32)
    return jnp.where(lax.broadcasted_iota(jnp.int32, total.shape, 0) == 0, total, second)


def kernel(
    tok_hbm, seg_hbm, gain_a_hbm, gain_f_hbm, wq_hbm, wk_hbm, wv_hbm, wo_hbm, wu_hbm, wd_hbm,
    o_ref,
    seg, gain_a, gain_f, wq, wk, wv, wo, wu, wd,
    tok, acc, ctx, part, sib, red, own_a, own_f, stats_a, stats_f, mu, scale, resid,
    nb, up, sb, land, act, part_down, down, fin,
    w_sem, ag_send, ag_recv, sib_send, sib_recv, red_send, red_recv, sa_send, sa_recv, sf_send, sf_recv,
    send, recv, nb_send, nb_recv, dp_send, dp_recv,
):
    a = lax.axis_index("section")
    t = lax.axis_index("tensor")
    d = lax.axis_index("dp")
    z, c = t // 2, t % 2
    xh, y = d // 4, d % 4
    oa, oc = 1 - a, 1 - c
    zp, zm, z2 = (z + 1) % 4, (z + 3) % 4, (z + 2) % 4
    me = a * 8 + t

    def dev(a_, z_, c_):
        return {"section": a_, "tensor": z_ * 2 + c_}

    def slot(a_, z_, c_):
        return a_ * 8 + z_ * 2 + c_

    def at_dp(d_):
        return {"dp": d_}

    def y_of(dy):
        return xh * 4 + (y + dy) % 4

    def peer(r):
        i = (me + r) % N_G
        return i, {"section": i // 8, "tensor": i % 8}

    D_X, D_ZP, D_ZM = dev(oa, z, c), dev(a, zp, c), dev(a, zm, c)
    D_Z2, D_S = dev(a, z2, c), dev(a, z, oc)
    across = (1 - xh) * 4 + y
    dp_peers = [at_dp(y_of(dy)) for dy in (1, 2, 3)] + [at_dp(across)]

    barrier = pltpu.get_barrier_semaphore()

    @pl.loop(1, N_G)
    def _(r):
        pl.semaphore_signal(barrier, inc=1, device_id=peer(r)[1], device_id_type=MESH)

    for device in dp_peers:
        pl.semaphore_signal(barrier, inc=1, device_id=device, device_id_type=MESH)

    pairs = (
        (tok_hbm, tok.at[me]), (gain_a_hbm, gain_a), (seg_hbm, seg), (gain_f_hbm.at[me], gain_f),
        (wq_hbm, wq), (wk_hbm, wk), (wv_hbm, wv), (wo_hbm, wo), (wu_hbm, wu), (wd_hbm, wd),
    )
    loads = [pltpu.make_async_copy(h, v, w_sem.at[n]) for n, (h, v) in enumerate(pairs)]
    for load in loads:
        load.start()
    loads[0].wait()
    for h in range(2):
        own_a[h] = partial_stats(tok[me, h])
    stats_a[me] = own_a[...]
    pl.semaphore_wait(barrier, N_G - 1 + len(dp_peers))

    sends = []

    def go(copy):
        copy.start()
        sends.append(copy)

    def stat_a(r):
        i, device = peer(r)
        return remote(own_a, stats_a.at[me], sa_send.at[r], sa_recv.at[me], device)

    def stat_f(h, r):
        i, device = peer(r)
        return remote(own_f.at[h], stats_f.at[h, me], sf_send.at[h, r], sf_recv.at[h, me], device)

    @pl.loop(1, N_G)
    def _(r):
        stat_a(r).start()

    def norm_from(total, h):
        mean = total[0:1] / 8192.0
        second = total[1:2] / 8192.0
        inverse = lax.rsqrt(second - mean * mean + 1e-05)
        mu[h] = rows_to_columns(mean, WIDE)
        scale[h] = rows_to_columns(inverse, WIDE)

    ags = []

    def ag(s, h, device):
        n = len(ags)
        ags.append(remote(tok.at[s, h], tok.at[s, h], ag_send.at[n], ag_recv.at[s, h], device))
        go(ags[n])

    def arrived(s, h):
        remote(tok.at[s, h], tok.at[s, h], ag_send.at[0], ag_recv.at[s, h], D_X).wait_recv()

    s_own, s_x, s_zp, s_zm = slot(a, z, c), slot(oa, z, c), slot(a, zp, c), slot(a, zm, c)
    s_z2, s_xzp, s_xzm, s_xz2 = slot(a, z2, c), slot(oa, zp, c), slot(oa, zm, c), slot(oa, z2, c)

    def other(s):
        return s + oc - c

    def project(s, h):
        x = (tok[s, h].astype(F32) - mu[h]) * scale[h] * gain_a[s]
        x = x.astype(BF16)
        at = pl.ds(pl.multiple_of(s * WIDE, WIDE), WIDE)
        for n, w in enumerate((wq, wk, wv)):
            acc[h, :, n * 256 : (n + 1) * 256] += jnp.dot(x, w[at, :], preferred_element_type=F32)

    def t_x(h):
        ag(s_own, h, D_X)

    def t_zz(h):
        ag(s_own, h, D_ZP)
        ag(s_own, h, D_ZM)

    def t_s(h):
        ag(s_own, h, D_S)

    def t_z2(h):
        ag(s_own, h, D_Z2)

    def t_fx(h):
        arrived(s_x, h)
        ag(s_x, h, D_ZP)
        ag(s_x, h, D_ZM)
        ag(s_x, h, D_S)

    def t_fz(h):
        for s in (s_zp, s_zm):
            arrived(s, h)
            ag(s, h, D_S)

    def t_f2(h):
        arrived(s_z2, h)
        ag(s_z2, h, D_X)
        ag(s_z2, h, D_S)

    def t_f3(h):
        for s in (s_xzp, s_xzm):
            arrived(s, h)
            ag(s, h, D_S)

    def t_f4(h):
        arrived(s_xz2, h)
        ag(s_xz2, h, D_S)

    def t_norm(h):
        if h == 0:

            @pl.loop(1, N_G)
            def _(r):
                i, device = peer(r)
                remote(own_a, stats_a.at[i], sa_send.at[r], sa_recv.at[i], device).wait_recv()

            for n in range(2):
                norm_from(jnp.sum(stats_a[:, n], axis=0), n)
            acc[...] = jnp.zeros_like(acc)
            for n in (1, 2, 3, 4, 5, 6):
                loads[n].wait()

    def t_p0(h):
        project(s_own, h)
        arrived(other(s_own), h)
        project(other(s_own), h)

    def t_px(h):
        project(s_x, h)

    def t_pz(h):
        project(s_zp, h)
        project(s_zm, h)

    def t_p2(h):
        project(s_z2, h)

    def t_p3(h):
        project(s_xzp, h)
        project(s_xzm, h)

    def t_p4(h):
        project(s_xz2, h)

    def others(h, *slots):
        for s in slots:
            arrived(other(s), h)
            project(other(s), h)

    def t_qx(h):
        others(h, s_x)

    def t_qz(h):
        others(h, s_zp, s_zm)

    def t_q2(h):
        others(h, s_z2)

    def t_q3(h):
        others(h, s_xzp, s_xzm)

    def t_q4(h):
        others(h, s_xz2)

    def t_att(h):
        keys = (h + 1) * HALF
        seg_row = seg[...].astype(F32)
        seg_col = rows_to_columns(seg_row[:, h * HALF : (h + 1) * HALF], keys)
        at_q = lax.broadcasted_iota(jnp.int32, (HALF, keys), 0) + h * HALF
        at_k = lax.broadcasted_iota(jnp.int32, (HALF, keys), 1)
        keep = jnp.logical_and(at_q >= at_k, seg_col == seg_row[:, :keys])
        for head in range(2):

            def part_of(n, halves):
                cols = slice(n * 256 + head * HD, n * 256 + (head + 1) * HD)
                return jnp.concatenate([acc[i, :, cols].astype(BF16) for i in halves], axis=0)

            q, k, v = part_of(0, (h,)), part_of(1, range(h + 1)), part_of(2, range(h + 1))
            scores = lax.dot_general(q, k, (((1,), (1,)), ((), ())), preferred_element_type=F32)
            scores = jnp.where(keep, scores * HD ** (-0.5), -1e30)
            expo = jnp.exp(scores - jnp.max(scores, axis=-1, keepdims=True))
            probs = (expo / jnp.sum(expo, axis=-1, keepdims=True)).astype(BF16)
            context = jnp.dot(probs, v, preferred_element_type=F32)
            ctx[h, :, head * HD : (head + 1) * HD] = context.astype(BF16)

    order = ((oa, z2), (oa, zp), (oa, zm), (a, zp), (a, zm), (a, z2), (oa, z), (a, z))

    def term(s, h):
        at = pl.ds(pl.multiple_of(s * WIDE, WIDE), WIDE)
        return jnp.dot(ctx[h], wo[:, at], preferred_element_type=F32)

    def sib_copy(n, h):
        return remote(part.at[oc, n, h], sib.at[n, h], sib_send.at[n, h], sib_recv.at[n, h], D_S)

    def t_opa(h):
        if h == 0:
            loads[7].wait()
        for n, (a_, z_) in enumerate(order):
            part[oc, n, h] = term(slot(a_, z_, oc), h).astype(BF16)
            go(sib_copy(n, h))

    red_to = (D_X, D_ZP, D_ZM, D_ZP, D_ZM, D_Z2, D_X)

    def red_copy(n, h):
        return remote(part.at[c, n, h], red.at[n, h], red_send.at[n, h], red_recv.at[n, h], red_to[n])

    def t_opb(h):
        for n, (a_, z_) in enumerate(order):
            mine = term(slot(a_, z_, c), h)
            sib_copy(n, h).wait_recv()
            part[c, n, h] = (mine + sib[n, h].astype(F32)).astype(BF16)
            if n < 5:
                go(red_copy(n, h))

    def add_landed(n, h, *landings):
        total = part[c, n, h].astype(F32)
        for i in landings:
            red_copy(i, h).wait_recv()
            total += red[i, h].astype(F32)
        return total

    def t_r1(h):
        part[c, 5, h] = add_landed(5, h, 0).astype(BF16)
        go(red_copy(5, h))

    def t_r1b(h):
        part[c, 6, h] = add_landed(6, h, 1, 2).astype(BF16)
        go(red_copy(6, h))

    def t_r3(h):
        total = tok[me, h].astype(F32) + add_landed(7, h, 3, 4, 6, 5)
        resid[h] = total.astype(BF16)
        own_f[h] = partial_stats(resid[h])
        stats_f[h, me] = own_f[h]

        @pl.loop(1, N_G)
        def _(r):
            stat_f(h, r).start()

    def nb_copy(n, h, s, device):
        return remote(nb.at[h, s], nb.at[h, s], nb_send.at[h, n], nb_recv.at[h, s], device)

    def nb_sends(h):
        to = (across, y_of(1), y_of(3), y_of(2))
        return [nb_copy(n, h, d, at_dp(d_)) for n, d_ in enumerate(to)]

    def nb_forwards(h):
        return [nb_copy(4 + n, h, across, at_dp(y_of(dy))) for n, dy in enumerate((1, 3, 2))]

    def nb_arrived(h, s):
        nb_copy(0, h, s, at_dp(across)).wait_recv()

    def t_nb(h):
        @pl.loop(1, N_G)
        def _(r):
            i, device = peer(r)
            remote(own_f.at[h], stats_f.at[h, i], sf_send.at[h, r], sf_recv.at[h, i], device).wait_recv()

        norm_from(jnp.sum(stats_f[h], axis=0), h)
        normed = (resid[h].astype(F32) - mu[h]) * scale[h] * gain_f[...]
        nb[h, d] = normed.astype(BF16)
        for copy in nb_sends(h):
            copy.start()

    def half_of(k):
        return pick(k, [h for h, r in CHUNKS])

    def replica_of(k):
        return pick(k, [r for h, r in CHUNKS])

    def block(k, a_, z_):
        return up.at[k % RING, c, a_ * 4 + z_]

    def act_block(k, a_, z_):
        return act.at[k, c, a_ * 4 + z_]

    def copy_of(kind, k):
        at = land.at[k]
        src, dst, device = {
            SB: lambda: (up.at[k % RING, oc], sb.at[k], D_S),
            RX1: lambda: (block(k, oa, z2), at.at[L_RX1], D_X),
            RZP: lambda: (block(k, oa, zp), at.at[L_RZP], D_ZP),
            RZM: lambda: (block(k, oa, zm), at.at[L_RZM], D_ZM),
            FX: lambda: (block(k, oa, z), at.at[L_FX], D_X),
            FZP1: lambda: (block(k, a, zp).at[1], at.at[L_FZP, 1], D_ZP),
            FZM0: lambda: (block(k, a, zm).at[0], at.at[L_FZM, 0], D_ZM),
            H0: lambda: (block(k, a, z2).at[0], at.at[L_H, 0], D_ZP),
            H1: lambda: (block(k, a, z2).at[1], at.at[L_H, 1], D_ZM),
            FZP0: lambda: (block(k, a, zp).at[0], at.at[L_FZP, 0], D_ZP),
            FZM1: lambda: (block(k, a, zm).at[1], at.at[L_FZM, 1], D_ZM),
            FZP: lambda: (block(k, a, zp), at.at[L_FZP], D_ZP),
            FZM: lambda: (block(k, a, zm), at.at[L_FZM], D_ZM),
            FZ2: lambda: (block(k, a, z2), at.at[L_H], D_Z2),
            AX: lambda: (act_block(k, a, z),) * 2 + (D_X,),
            AZP: lambda: (act_block(k, a, z),) * 2 + (D_ZP,),
            AZM: lambda: (act_block(k, a, z),) * 2 + (D_ZM,),
            AZ2: lambda: (act_block(k, a, z),) * 2 + (D_Z2,),
            XZP: lambda: (act_block(k, oa, z),) * 2 + (D_ZP,),
            XZM: lambda: (act_block(k, oa, z),) * 2 + (D_ZM,),
            XZ2: lambda: (act_block(k, a, z2),) * 2 + (D_X,),
            ZH0: lambda: (act_block(k, a, zm).at[0],) * 2 + (D_ZP,),
            ZH1: lambda: (act_block(k, a, zp).at[1],) * 2 + (D_ZM,),
            AS: lambda: (act.at[k, c],) * 2 + (D_S,),
        }[kind]()
        return remote(src, dst, send.at[k, kind], recv.at[k, kind], device)

    def got(k, *kinds):
        for kind in kinds:
            if kind < AX:
                copy_of(kind, k).wait_recv()
                continue
            ref = {
                AX: lambda: act_block(k, oa, z),
                AZP: lambda: act_block(k, a, zm),
                AZM: lambda: act_block(k, a, zp),
                AZ2: lambda: act_block(k, a, z2),
                XZP: lambda: act_block(k, oa, zm),
                XZM: lambda: act_block(k, oa, zp),
                XZ2: lambda: act_block(k, oa, z2),
                ZH0: lambda: act_block(k, a, z2).at[0],
                ZH1: lambda: act_block(k, a, z2).at[1],
                AS: lambda: act.at[k, oc],
            }[kind]()
            remote(ref, ref, send.at[k, kind], recv.at[k, kind], D_X).wait_recv()

    def give(k, *kinds):
        for kind in kinds:
            copy_of(kind, k).start()

    def either(condition, yes, no):
        pl.when(condition)(yes)
        pl.when(jnp.logical_not(condition))(no)

    def gave(k, *kinds):
        for kind in kinds:
            copy_of(kind, k).wait_send()

    def sums_sent(k):
        gave(k, SB, RX1, RZP, RZM, FX)
        either(
            k < DIRECT_SUM,
            lambda: gave(k, FZP, FZM, FZ2),
            lambda: gave(k, FZP1, FZM0, H0, H1, FZP0, FZM1),
        )

    def up_product(k):
        h, r = half_of(k), replica_of(k)
        s = ((xh + r // 4) % 2) * 4 + (y + r % 4) % 4
        for n in range(2):

            @pl.when(k == FORWARD_AT[n])
            def _():
                nb_arrived(n, across)
                for copy in nb_forwards(n):
                    copy.start()

        @pl.when(pick(k, [int(r_ not in (0, 4)) for _, r_ in CHUNKS]) == 1)
        def _():
            nb_arrived(h, s)

        @pl.when(k >= RING)
        def _():
            sums_sent(k - RING)

        x = nb[h, s]
        for n in range(4):
            r_ = jnp.dot(x, wu[:, n * 512 : (n + 1) * 512], preferred_element_type=F32)
            up[k % RING, n // 2, :, n % 2] = r_.astype(BF16).reshape(8, 16, 512)
        give(k, SB)

    def pair_sum(k):
        got(k, SB)
        i = k % RING
        up[i, c] = (up[i, c].astype(F32) + sb[k].astype(F32)).astype(BF16)
        give(k, RX1, RZP, RZM)
        either(k < DIRECT_SUM, lambda: give(k, FZP, FZM), lambda: give(k, FZP1, FZM0))

    def second_sum(k):
        i = k % RING
        got(k, RX1)
        b = a * 4 + z2
        up[i, c, b] = (up[i, c, b].astype(F32) + land[k, L_RX1].astype(F32)).astype(BF16)
        either(k < DIRECT_SUM, lambda: give(k, FZ2), lambda: give(k, H0, H1))
        got(k, RZP, RZM)
        b = oa * 4 + z
        both = land[k, L_RZP].astype(F32) + land[k, L_RZM].astype(F32)
        up[i, c, b] = (up[i, c, b].astype(F32) + both).astype(BF16)
        give(k, FX)

    def third_sum(k):
        i = k % RING

        @pl.when(k >= DIRECT_SUM)
        def _():
            for kind, then, z_, half in ((H0, FZP0, zp, 0), (H1, FZM1, zm, 1)):
                got(k, kind)
                b = a * 4 + z_
                both = up[i, c, b, half].astype(F32) + land[k, L_H, half].astype(F32)
                up[i, c, b, half] = both.astype(BF16)
                give(k, then)

    def activate(k):
        i, b = k % RING, a * 4 + z

        def finish(pre, *landings):
            for n in landings:
                pre += land[k, n].astype(F32)
            inner = 0.7978845608028654 * (pre + 0.044715 * (pre * pre * pre))
            act[k, c, b] = (0.5 * pre * (1.0 + jnp.tanh(inner))).astype(BF16)

        def from_four():
            got(k, FZP, FZM, FX, FZ2)
            finish(up[i, c, b].astype(F32), L_FZP, L_FZM, L_FX, L_H)

        def from_three():
            got(k, FZP1, FZM0, FX, FZP0, FZM1)
            finish(up[i, c, b].astype(F32), L_FZP, L_FZM, L_FX)

        either(k < DIRECT_SUM, from_four, from_three)

        @pl.when(k >= DIRECT_GATHER)
        def _():
            give(k, AZ2)

        give(k, AX, AZP, AZM)

    def spread(k):
        got(k, AX)
        give(k, XZP, XZM)

        def direct():
            got(k, AZ2)
            give(k, XZ2)

        def halves():
            got(k, AZP)
            give(k, ZH0)
            got(k, AZM)
            give(k, ZH1)

        either(k >= DIRECT_GATHER, direct, halves)

    def spread_across(k):
        def halves():
            got(k, ZH0, ZH1)
            give(k, XZ2)

        either(k >= DIRECT_GATHER, lambda: got(k, AZP, AZM), halves)

    def down_half(k, c_):
        r = jnp.zeros((HALF, WIDE), F32)
        for q in range(2):
            x = act[k, c_, :, q].reshape(HALF, 512)
            r += jnp.dot(x, wd[c_ * 2 + q], preferred_element_type=F32)
        return r

    def to_sibling(k):
        got(k, XZP, XZM, XZ2)
        give(k, AS)
        part_down[...] = down_half(k, c)

    def dp_copy(k):
        r = replica_of(k)
        x_ = (xh + pick(k, [int(r_ == 4) for _, r_ in CHUNKS])) % 2
        to = at_dp(x_ * 4 + (y + r % 4) % 4)
        return remote(down.at[k], fin.at[half_of(k), r], dp_send.at[k], dp_recv.at[half_of(k), r], to)

    def fin_arrived(h, r):
        remote(down.at[0], fin.at[h, r], dp_send.at[0], dp_recv.at[h, r], at_dp(across)).wait_recv()

    def is_sent(k):
        return pick(k, [int(r_ != 0) for _, r_ in CHUNKS]) == 1

    def down_product(k):
        got(k, AS)
        down[k] = (part_down[...] + down_half(k, oc)).astype(BF16)
        for h in range(2):

            @pl.when(k == CHUNK_OF[h, 4])
            def _():
                total = down[k].astype(F32)
                for r in (5, 6, 7):
                    fin_arrived(h, r)
                    total += fin[h, r].astype(F32)
                down[k] = total.astype(BF16)

        @pl.when(is_sent(k))
        def _():
            dp_copy(k).start()

    tasks = {name[2:]: f for name, f in locals().items() if name.startswith("t_")}
    for name, h in (
        ("s", 0), ("z2", 0), ("x", 0), ("zz", 0), ("x", 1), ("fx", 0), ("z2", 1), ("f2", 0), ("fz", 0),
        ("norm", 0), ("px", 0), ("qz", 0), ("qx", 0), ("q2", 0), ("fx", 1), ("f3", 0), ("p3", 0), ("zz", 1),
        ("f4", 0), ("p0", 0), ("q3", 0), ("p4", 0), ("q4", 0), ("pz", 0), ("p2", 0), ("f2", 1), ("att", 0),
        ("s", 1), ("px", 1), ("opa", 0), ("opb", 0), ("p2", 1), ("f3", 1), ("f4", 1), ("p4", 1), ("q2", 1),
        ("p0", 1), ("fz", 1), ("pz", 1), ("r1", 0), ("r1b", 0), ("q3", 1), ("qx", 1), ("qz", 1), ("q4", 1),
        ("p3", 1), ("att", 1), ("opa", 1), ("r3", 0), ("opb", 1), ("nb", 0),
    ):
        tasks[name](h)
    loads[8].wait()
    loads[9].wait()
    up_product(0)
    t_r1(1)
    t_r1b(1)

    @pl.loop(0, N_K + 7)
    def _(step):
        pl.when(step == 2)(lambda: t_r3(1))
        pl.when(step == 4)(lambda: t_nb(1))
        for f, lag in (
            (pair_sum, 0), (up_product, -1), (second_sum, 1), (third_sum, 2), (down_product, 7),
            (activate, 3), (to_sibling, 6), (spread, 4), (spread_across, 5),
        ):
            k = step - lag
            pl.when(jnp.logical_and(k >= 0, k < N_K))(lambda f=f, k=k: f(k))

    for h in range(2):
        total = resid[h].astype(F32) + down[CHUNK_OF[h, 0]].astype(F32)
        for r in (1, 2, 3, 4):
            fin_arrived(h, r)
            total += fin[h, r].astype(F32)
        o_ref[h] = total.astype(BF16)

    for copy in sends:
        copy.wait_send()
    for h in range(2):
        for copy in nb_sends(h) + nb_forwards(h):
            copy.wait_send()

    @pl.loop(1, N_G)
    def _(r):
        stat_a(r).wait_send()
        stat_f(0, r).wait_send()
        stat_f(1, r).wait_send()

    @pl.loop(N_K - RING, N_K)
    def _(k):
        sums_sent(k)

    @pl.loop(0, N_K)
    def _(k):
        gave(k, AX, AZP, AZM, XZP, XZM, XZ2, AS)
        either(k >= DIRECT_GATHER, lambda: gave(k, AZ2), lambda: gave(k, ZH0, ZH1))
        pl.when(is_sent(k))(lambda: dp_copy(k).wait_send())


def per_device(
    tokens, segment_ids, gain_attn, w_query, w_key, w_value, w_output, gain_ffn, w_up, w_down
):
    rows, share = tokens.shape
    vmem, hbm = pl.BlockSpec(memory_space=pltpu.VMEM), pl.BlockSpec(memory_space=pl.ANY)
    half = (HALF, share)
    dma = pltpu.SemaphoreType.DMA

    def b(*shape):
        return pltpu.VMEM(shape, BF16)

    def f(*shape):
        return pltpu.VMEM(shape, F32)

    out = pl.pallas_call(
        kernel,
        out_shape=jax.ShapeDtypeStruct((2, *half), BF16),
        in_specs=[hbm] * 10,
        out_specs=vmem,
        scratch_shapes=[
            pltpu.VMEM(segment_ids.shape, jnp.int32), f(N_G, 1, share), f(1, share),
            b(*w_query.shape), b(*w_query.shape), b(*w_query.shape), b(*w_output.shape),
            b(*w_up.shape), b(4, 512, share),
            b(N_G, 2, *half), f(2, HALF, 768), b(2, HALF, 256), b(2, 8, 2, *half), b(8, 2, *half),
            b(7, 2, *half), f(2, 8, HALF), f(2, 8, HALF), f(N_G, 2, 8, HALF), f(2, N_G, 8, HALF),
            f(2, *half), f(2, *half), b(2, *half),
            b(2, N_DP, *half), b(RING, 2, 8, 2, 16, 512), b(N_K, 8, 2, 16, 512), b(N_K, 7, 2, 16, 512),
            b(N_K, 2, 8, 2, 16, 512), f(*half), b(N_K, *half), b(2, N_DP, *half),
            dma((10,)), dma((30,)), dma((N_G, 2)), dma((8, 2)), dma((8, 2)), dma((7, 2)), dma((7, 2)),
            dma((N_G,)), dma((N_G,)), dma((2, N_G)), dma((2, N_G)),
            dma((N_K, KINDS)), dma((N_K, KINDS)), dma((2, 7)), dma((2, N_DP)), dma((N_K,)), dma((2, N_DP)),
        ],
        compiler_params=pltpu.CompilerParams(
            collective_id=0, has_side_effects=True, vmem_limit_bytes=62 << 20
        ),
        name="layer",
    )(
        tokens.reshape(2, *half), segment_ids, gain_attn.reshape(N_G, 1, share),
        gain_ffn.reshape(N_G, 1, share), w_query, w_key, w_value, w_output, w_up,
        w_down.reshape(4, 512, share),
    )
    return out.reshape(rows, share)


def solution(mesh):
    return jax.shard_map(
        per_device,
        mesh=mesh,
        in_specs=(
            P("dp", ("section", "tensor")),
            P("dp", None),
            P(),
            P(None, ("section", "tensor")),
            P(None, ("section", "tensor")),
            P(None, ("section", "tensor")),
            P(("section", "tensor"), None),
            P(),
            P(("section", "tensor"), "dp"),
            P("dp", ("section", "tensor")),
        ),
        out_specs=P("dp", ("section", "tensor")),
        check_vma=False,
    )
```

```python
import jax
import jax.numpy as jnp
from jax import lax
from jax.experimental import pallas as pl
from jax.experimental.pallas import tpu as pltpu
from jax.sharding import PartitionSpec as P

MESH = pl.DeviceIdType.MESH
HD = 128
F32 = jnp.float32
BF16 = jnp.bfloat16
N_G = 16
N_DP = 8
HALF = 128
WIDE = 512

CHUNKS = (
    (0, 0), (0, 3), (0, 1), (0, 2), (0, 7), (0, 6), (1, 3), (1, 1),
    (0, 5), (1, 7), (1, 6), (1, 5), (0, 4), (1, 2), (1, 4), (1, 0),
)
N_K = len(CHUNKS)
CHUNK_OF = {chunk: k for k, chunk in enumerate(CHUNKS)}
FORWARD_AT = (2, 7)
DIRECT_SUM = 6
DIRECT_GATHER = 11
RING = 8

(
    SB, RX1, RZP, RZM, FX, FZP1, FZM0, H0, H1, FZP0, FZM1, FZP, FZM, FZ2,
    AX, AZP, AZM, XZP, XZM, XZ2, AS, ZH0, ZH1, AZ2,
) = range(24)
GROUPS = (
    (SB,), (RX1,), (RZP, RZM), (FX, FZP1, FZM0, FZP0, FZM1, FZP, FZM, FZ2), (H0,), (H1,),
    (AX,), (AZP,), (AZM,), (XZP, XZM, XZ2), (AS,), (ZH0, ZH1, AZ2),
)
GROUP_OF = {kind: n for n, group in enumerate(GROUPS) for kind in group}
L_RX1, L_RZP, L_RZM, L_FX, L_FZP, L_FZM, L_H = range(7)
BLOCKS = 15


def remote(src, dst, send_sem, recv_sem, device):
    return pltpu.make_async_remote_copy(
        src_ref=src,
        dst_ref=dst,
        send_sem=send_sem,
        recv_sem=recv_sem,
        device_id=device,
        device_id_type=MESH,
    )


def pick(k, values):
    result = jnp.int32(values[0])
    for i, value in enumerate(values[1:], 1):
        result = jnp.where(k == i, jnp.int32(value), result)
    return result


def rows_to_columns(row, width):
    column = jnp.transpose(jnp.broadcast_to(row, (128, row.shape[1])))
    return jnp.concatenate([column] * (width // 128), axis=1)


def partial_stats(values):
    ones = jnp.ones((8, values.shape[1]), BF16)
    dims = (((1,), (1,)), ((), ()))
    wide = values.astype(F32)
    square = wide * wide
    high = square.astype(BF16)
    low = (square - high.astype(F32)).astype(BF16)
    total = lax.dot_general(ones, values, dims, preferred_element_type=F32)
    second = lax.dot_general(ones, high, dims, preferred_element_type=F32)
    second += lax.dot_general(ones, low, dims, preferred_element_type=F32)
    return jnp.where(lax.broadcasted_iota(jnp.int32, total.shape, 0) == 0, total, second)


def kernel(
    tok_hbm, seg_hbm, gain_a_hbm, gain_f_hbm, wq_hbm, wk_hbm, wv_hbm, wo_hbm, wu_hbm, wd_hbm,
    o_ref,
    seg, gain_a, gain_f, wq, wk, wv, wo, wu, wd,
    tok, acc, ctx, part, sib, red, own_a, own_f, stats_a, stats_f, mu, scale, resid,
    nb, up, sb, land, act, part_down, down, fin,
    w_sem, ag_send, ag_recv, sib_send, sib_recv, red_send, red_recv, sa_send, sa_recv, sf_send, sf_recv,
    sum_send, act_send, recv, nb_send, nb_recv, dp_send, dp_recv,
):
    a = lax.axis_index("section")
    t = lax.axis_index("tensor")
    d = lax.axis_index("dp")
    z, c = t // 2, t % 2
    xh, y = d // 4, d % 4
    oa, oc = 1 - a, 1 - c
    zp, zm, z2 = (z + 1) % 4, (z + 3) % 4, (z + 2) % 4
    me = a * 8 + t

    def dev(a_, z_, c_):
        return {"section": a_, "tensor": z_ * 2 + c_}

    def slot(a_, z_, c_):
        return a_ * 8 + z_ * 2 + c_

    def at_dp(d_):
        return {"dp": d_}

    def y_of(dy):
        return xh * 4 + (y + dy) % 4

    def peer(r):
        i = (me + r) % N_G
        return i, {"section": i // 8, "tensor": i % 8}

    D_X, D_ZP, D_ZM = dev(oa, z, c), dev(a, zp, c), dev(a, zm, c)
    D_Z2, D_S = dev(a, z2, c), dev(a, z, oc)
    across = (1 - xh) * 4 + y
    dp_peers = [at_dp(y_of(dy)) for dy in (1, 2, 3)] + [at_dp(across)]

    barrier = pltpu.get_barrier_semaphore()

    @pl.loop(1, N_G)
    def _(r):
        pl.semaphore_signal(barrier, inc=1, device_id=peer(r)[1], device_id_type=MESH)

    for device in dp_peers:
        pl.semaphore_signal(barrier, inc=1, device_id=device, device_id_type=MESH)

    pairs = (
        (tok_hbm, tok.at[me]), (gain_a_hbm, gain_a), (seg_hbm, seg), (gain_f_hbm.at[me], gain_f),
        (wq_hbm, wq), (wk_hbm, wk), (wv_hbm, wv), (wo_hbm, wo), (wu_hbm, wu), (wd_hbm, wd),
    )
    loads = [pltpu.make_async_copy(h, v, w_sem.at[n]) for n, (h, v) in enumerate(pairs)]
    for load in loads:
        load.start()
    loads[0].wait()
    for h in range(2):
        own_a[h] = partial_stats(tok[me, h])
    stats_a[0] = own_a[...]
    pl.semaphore_wait(barrier, N_G - 1 + len(dp_peers))

    def stat_a(r):
        i, device = peer(r)
        return remote(own_a, stats_a.at[r], sa_send.at[0], sa_recv.at[0], device)

    def stat_f(h, r):
        i, device = peer(r)
        return remote(own_f.at[h], stats_f.at[h, r], sf_send.at[h], sf_recv.at[h], device)

    def all_of(ref, send_sem, recv_sem):
        return remote(ref, ref, send_sem, recv_sem, D_X)

    others_a = all_of(stats_a.at[pl.ds(1, N_G - 1)], sa_send.at[0], sa_recv.at[0])
    others_f = [all_of(stats_f.at[h, pl.ds(1, N_G - 1)], sf_send.at[h], sf_recv.at[h]) for h in range(2)]

    @pl.loop(1, N_G)
    def _(r):
        stat_a(r).start()

    def norm_from(total, h):
        mean = total[0:1] / 8192.0
        second = total[1:2] / 8192.0
        inverse = lax.rsqrt(second - mean * mean + 1e-05)
        mu[h] = rows_to_columns(mean, WIDE)
        scale[h] = rows_to_columns(inverse, WIDE)

    def ag(s, h, device):
        remote(tok.at[s, h], tok.at[s, h], ag_send.at[0], ag_recv.at[s, h], device).start()

    def arrived(s, h):
        remote(tok.at[s, h], tok.at[s, h], ag_send.at[0], ag_recv.at[s, h], D_X).wait_recv()

    s_own, s_x, s_zp, s_zm = slot(a, z, c), slot(oa, z, c), slot(a, zp, c), slot(a, zm, c)
    s_z2, s_xzp, s_xzm, s_xz2 = slot(a, z2, c), slot(oa, zp, c), slot(oa, zm, c), slot(oa, z2, c)

    def other(s):
        return s + oc - c

    def project(s, h):
        x = (tok[s, h].astype(F32) - mu[h]) * scale[h] * gain_a[s]
        x = x.astype(BF16)
        at = pl.ds(pl.multiple_of(s * WIDE, WIDE), WIDE)
        for n, w in enumerate((wq, wk, wv)):
            acc[h, :, n * 256 : (n + 1) * 256] += jnp.dot(x, w[at, :], preferred_element_type=F32)

    def t_x(h):
        ag(s_own, h, D_X)

    def t_zz(h):
        ag(s_own, h, D_ZP)
        ag(s_own, h, D_ZM)

    def t_s(h):
        ag(s_own, h, D_S)

    def t_z2(h):
        ag(s_own, h, D_Z2)

    def t_fx(h):
        arrived(s_x, h)
        ag(s_x, h, D_ZP)
        ag(s_x, h, D_ZM)
        ag(s_x, h, D_S)

    def t_fz(h):
        for s in (s_zp, s_zm):
            arrived(s, h)
            ag(s, h, D_S)

    def t_f2(h):
        arrived(s_z2, h)
        ag(s_z2, h, D_X)
        ag(s_z2, h, D_S)

    def t_f3(h):
        for s in (s_xzp, s_xzm):
            arrived(s, h)
            ag(s, h, D_S)

    def t_f4(h):
        arrived(s_xz2, h)
        ag(s_xz2, h, D_S)

    def t_norm(h):
        if h == 0:

            others_a.wait_recv()
            for n in range(2):
                norm_from(jnp.sum(stats_a[:, n], axis=0), n)
            acc[...] = jnp.zeros_like(acc)
            for n in (1, 2, 3, 4, 5, 6):
                loads[n].wait()

    def t_p0(h):
        project(s_own, h)
        arrived(other(s_own), h)
        project(other(s_own), h)

    def t_px(h):
        project(s_x, h)

    def t_pz(h):
        project(s_zp, h)
        project(s_zm, h)

    def t_p2(h):
        project(s_z2, h)

    def t_p3(h):
        project(s_xzp, h)
        project(s_xzm, h)

    def t_p4(h):
        project(s_xz2, h)

    def others(h, *slots):
        for s in slots:
            arrived(other(s), h)
            project(other(s), h)

    def t_qx(h):
        others(h, s_x)

    def t_qz(h):
        others(h, s_zp, s_zm)

    def t_q2(h):
        others(h, s_z2)

    def t_q3(h):
        others(h, s_xzp, s_xzm)

    def t_q4(h):
        others(h, s_xz2)

    def t_att(h):
        keys = (h + 1) * HALF
        seg_row = seg[...].astype(F32)
        seg_col = rows_to_columns(seg_row[:, h * HALF : (h + 1) * HALF], keys)
        at_q = lax.broadcasted_iota(jnp.int32, (HALF, keys), 0) + h * HALF
        at_k = lax.broadcasted_iota(jnp.int32, (HALF, keys), 1)
        keep = jnp.logical_and(at_q >= at_k, seg_col == seg_row[:, :keys])
        for head in range(2):

            def part_of(n, halves):
                cols = slice(n * 256 + head * HD, n * 256 + (head + 1) * HD)
                return jnp.concatenate([acc[i, :, cols].astype(BF16) for i in halves], axis=0)

            q, k, v = part_of(0, (h,)), part_of(1, range(h + 1)), part_of(2, range(h + 1))
            scores = lax.dot_general(q, k, (((1,), (1,)), ((), ())), preferred_element_type=F32)
            scores = jnp.where(keep, scores * HD ** (-0.5), -1e30)
            expo = jnp.exp(scores - jnp.max(scores, axis=-1, keepdims=True))
            probs = (expo / jnp.sum(expo, axis=-1, keepdims=True)).astype(BF16)
            context = jnp.dot(probs, v, preferred_element_type=F32)
            ctx[h, :, head * HD : (head + 1) * HD] = context.astype(BF16)

    order = ((oa, z2), (oa, zp), (oa, zm), (a, zp), (a, zm), (a, z2), (oa, z), (a, z))

    def term(s, h):
        at = pl.ds(pl.multiple_of(s * WIDE, WIDE), WIDE)
        return jnp.dot(ctx[h], wo[:, at], preferred_element_type=F32)

    def sib_copy(n, h):
        return remote(part.at[oc, n, h], sib.at[n, h], sib_send.at[0], sib_recv.at[n, h], D_S)

    def t_opa(h):
        if h == 0:
            loads[7].wait()
        for n, (a_, z_) in enumerate(order):
            part[oc, n, h] = term(slot(a_, z_, oc), h).astype(BF16)
            sib_copy(n, h).start()

    red_to = (D_X, D_ZP, D_ZM, D_ZP, D_ZM, D_Z2, D_X)

    def red_copy(n, h):
        return remote(part.at[c, n, h], red.at[n, h], red_send.at[0], red_recv.at[n, h], red_to[n])

    def t_opb(h):
        for n, (a_, z_) in enumerate(order):
            mine = term(slot(a_, z_, c), h)
            sib_copy(n, h).wait_recv()
            part[c, n, h] = (mine + sib[n, h].astype(F32)).astype(BF16)
            if n < 5:
                red_copy(n, h).start()

    def add_landed(n, h, *landings):
        total = part[c, n, h].astype(F32)
        for i in landings:
            red_copy(i, h).wait_recv()
            total += red[i, h].astype(F32)
        return total

    def t_r1(h):
        part[c, 5, h] = add_landed(5, h, 0).astype(BF16)
        red_copy(5, h).start()

    def t_r1b(h):
        part[c, 6, h] = add_landed(6, h, 1, 2).astype(BF16)
        red_copy(6, h).start()

    def t_r3(h):
        total = tok[me, h].astype(F32) + add_landed(7, h, 3, 4, 6, 5)
        resid[h] = total.astype(BF16)
        own_f[h] = partial_stats(resid[h])
        stats_f[h, 0] = own_f[h]

        @pl.loop(1, N_G)
        def _(r):
            stat_f(h, r).start()

    def nb_copy(h, s, device):
        return remote(nb.at[h, s], nb.at[h, s], nb_send.at[h], nb_recv.at[h, s], device)

    def nb_sends(h):
        to = (across, y_of(1), y_of(3), y_of(2))
        return [nb_copy(h, d, at_dp(d_)) for d_ in to]

    def nb_forwards(h):
        return [nb_copy(h, across, at_dp(y_of(dy))) for dy in (1, 3, 2)]

    def nb_arrived(h, s):
        nb_copy(h, s, at_dp(across)).wait_recv()

    def t_nb(h):
        others_f[h].wait_recv()
        norm_from(jnp.sum(stats_f[h], axis=0), h)
        normed = (resid[h].astype(F32) - mu[h]) * scale[h] * gain_f[...]
        nb[h, d] = normed.astype(BF16)
        for copy in nb_sends(h):
            copy.start()

    def half_of(k):
        return pick(k, [h for h, r in CHUNKS])

    def replica_of(k):
        return pick(k, [r for h, r in CHUNKS])

    def block(k, a_, z_):
        return up.at[k % RING, c, a_ * 4 + z_]

    def act_block(k, a_, z_):
        return act.at[k, c, a_ * 4 + z_]

    def copy_of(kind, k):
        at = land.at[k]
        src, dst, device = {
            SB: lambda: (up.at[k % RING, oc], sb.at[k], D_S),
            RX1: lambda: (block(k, oa, z2), at.at[L_RX1], D_X),
            RZP: lambda: (block(k, oa, zp), at.at[L_RZP], D_ZP),
            RZM: lambda: (block(k, oa, zm), at.at[L_RZM], D_ZM),
            FX: lambda: (block(k, oa, z), at.at[L_FX], D_X),
            FZP1: lambda: (block(k, a, zp).at[1], at.at[L_FZP, 1], D_ZP),
            FZM0: lambda: (block(k, a, zm).at[0], at.at[L_FZM, 0], D_ZM),
            H0: lambda: (block(k, a, z2).at[0], at.at[L_H, 0], D_ZP),
            H1: lambda: (block(k, a, z2).at[1], at.at[L_H, 1], D_ZM),
            FZP0: lambda: (block(k, a, zp).at[0], at.at[L_FZP, 0], D_ZP),
            FZM1: lambda: (block(k, a, zm).at[1], at.at[L_FZM, 1], D_ZM),
            FZP: lambda: (block(k, a, zp), at.at[L_FZP], D_ZP),
            FZM: lambda: (block(k, a, zm), at.at[L_FZM], D_ZM),
            FZ2: lambda: (block(k, a, z2), at.at[L_H], D_Z2),
            AX: lambda: (act_block(k, a, z),) * 2 + (D_X,),
            AZP: lambda: (act_block(k, a, z),) * 2 + (D_ZP,),
            AZM: lambda: (act_block(k, a, z),) * 2 + (D_ZM,),
            AZ2: lambda: (act_block(k, a, z),) * 2 + (D_Z2,),
            XZP: lambda: (act_block(k, oa, z),) * 2 + (D_ZP,),
            XZM: lambda: (act_block(k, oa, z),) * 2 + (D_ZM,),
            XZ2: lambda: (act_block(k, a, z2),) * 2 + (D_X,),
            ZH0: lambda: (act_block(k, a, zm).at[0],) * 2 + (D_ZP,),
            ZH1: lambda: (act_block(k, a, zp).at[1],) * 2 + (D_ZM,),
            AS: lambda: (act.at[k, c],) * 2 + (D_S,),
        }[kind]()
        sent = sum_send.at[k % RING] if kind < AX else act_send.at[0]
        return remote(src, dst, sent, recv.at[k % RING, GROUP_OF[kind]], device)

    def got(k, kind, ref):
        all_of(ref, act_send.at[0], recv.at[k % RING, GROUP_OF[kind]]).wait_recv()

    def give(k, *kinds):
        for kind in kinds:
            copy_of(kind, k).start()

    def either(condition, yes, no):
        pl.when(condition)(yes)
        pl.when(jnp.logical_not(condition))(no)

    def sums_sent(k):
        i = k % RING
        all_of(act.at[pl.ds(0, BLOCKS), 0, 0], sum_send.at[i], recv.at[0, 0]).wait_send()

    def up_product(k):
        h, r = half_of(k), replica_of(k)
        s = ((xh + r // 4) % 2) * 4 + (y + r % 4) % 4
        for n in range(2):

            @pl.when(k == FORWARD_AT[n])
            def _():
                nb_arrived(n, across)
                for copy in nb_forwards(n):
                    copy.start()

        @pl.when(pick(k, [int(r_ not in (0, 4)) for _, r_ in CHUNKS]) == 1)
        def _():
            nb_arrived(h, s)

        @pl.when(k >= RING)
        def _():
            sums_sent(k - RING)

        x = nb[h, s]
        for n in range(4):
            r_ = jnp.dot(x, wu[:, n * 512 : (n + 1) * 512], preferred_element_type=F32)
            up[k % RING, n // 2, :, n % 2] = r_.astype(BF16).reshape(8, 16, 512)
        give(k, SB)

    def pair_sum(k):
        got(k, SB, sb.at[k])
        i = k % RING
        up[i, c] = (up[i, c].astype(F32) + sb[k].astype(F32)).astype(BF16)
        give(k, RX1, RZP, RZM)
        either(k < DIRECT_SUM, lambda: give(k, FZP, FZM), lambda: give(k, FZP1, FZM0))

    def second_sum(k):
        i = k % RING
        got(k, RX1, land.at[k, L_RX1])
        b = a * 4 + z2
        up[i, c, b] = (up[i, c, b].astype(F32) + land[k, L_RX1].astype(F32)).astype(BF16)
        either(k < DIRECT_SUM, lambda: give(k, FZ2), lambda: give(k, H0, H1))
        got(k, RZP, land.at[k, pl.ds(L_RZP, 2)])
        b = oa * 4 + z
        both = land[k, L_RZP].astype(F32) + land[k, L_RZM].astype(F32)
        up[i, c, b] = (up[i, c, b].astype(F32) + both).astype(BF16)
        give(k, FX)

    def third_sum(k):
        i = k % RING

        @pl.when(k >= DIRECT_SUM)
        def _():
            for kind, then, z_, half in ((H0, FZP0, zp, 0), (H1, FZM1, zm, 1)):
                got(k, kind, land.at[k, L_H, half])
                b = a * 4 + z_
                both = up[i, c, b, half].astype(F32) + land[k, L_H, half].astype(F32)
                up[i, c, b, half] = both.astype(BF16)
                give(k, then)

    def activate(k):
        i, b = k % RING, a * 4 + z

        def finish(pre, *landings):
            for n in landings:
                pre += land[k, n].astype(F32)
            inner = 0.7978845608028654 * (pre + 0.044715 * (pre * pre * pre))
            act[k, c, b] = (0.5 * pre * (1.0 + jnp.tanh(inner))).astype(BF16)

        def from_four():
            got(k, FX, land.at[k, pl.ds(L_FX, 4)])
            finish(up[i, c, b].astype(F32), L_FZP, L_FZM, L_FX, L_H)

        def from_three():
            got(k, FX, land.at[k, pl.ds(L_FX, 3)])
            finish(up[i, c, b].astype(F32), L_FZP, L_FZM, L_FX)

        either(k < DIRECT_SUM, from_four, from_three)

        @pl.when(k >= DIRECT_GATHER)
        def _():
            give(k, AZ2)

        give(k, AX, AZP, AZM)

    def spread(k):
        got(k, AX, act_block(k, oa, z))
        give(k, XZP, XZM)

        def direct():
            got(k, AZ2, act_block(k, a, z2))
            give(k, XZ2)

        def halves():
            got(k, AZP, act_block(k, a, zm))
            give(k, ZH0)
            got(k, AZM, act_block(k, a, zp))
            give(k, ZH1)

        either(k >= DIRECT_GATHER, direct, halves)

    def spread_across(k):
        def halves():
            got(k, ZH0, act_block(k, a, z2))
            give(k, XZ2)

        def direct():
            got(k, AZP, act_block(k, a, zm))
            got(k, AZM, act_block(k, a, zp))

        either(k >= DIRECT_GATHER, direct, halves)

    def down_half(k, c_):
        r = jnp.zeros((HALF, WIDE), F32)
        for q in range(2):
            x = act[k, c_, :, q].reshape(HALF, 512)
            r += jnp.dot(x, wd[c_ * 2 + q], preferred_element_type=F32)
        return r

    def to_sibling(k):
        got(k, XZP, act.at[k, c, pl.ds(0, 3)])
        give(k, AS)
        part_down[...] = down_half(k, c)

    def dp_copy(k):
        r = replica_of(k)
        x_ = (xh + pick(k, [int(r_ == 4) for _, r_ in CHUNKS])) % 2
        to = at_dp(x_ * 4 + (y + r % 4) % 4)
        return remote(down.at[k], fin.at[half_of(k), r], dp_send.at[0], dp_recv.at[half_of(k), r], to)

    def fin_arrived(h, r):
        remote(down.at[0], fin.at[h, r], dp_send.at[0], dp_recv.at[h, r], at_dp(across)).wait_recv()

    def is_sent(k):
        return pick(k, [int(r_ != 0) for _, r_ in CHUNKS]) == 1

    def down_product(k):
        got(k, AS, act.at[k, oc])
        down[k] = (part_down[...] + down_half(k, oc)).astype(BF16)
        for h in range(2):

            @pl.when(k == CHUNK_OF[h, 4])
            def _():
                total = down[k].astype(F32)
                for r in (5, 6, 7):
                    fin_arrived(h, r)
                    total += fin[h, r].astype(F32)
                down[k] = total.astype(BF16)

        @pl.when(is_sent(k))
        def _():
            dp_copy(k).start()

    tasks = {name[2:]: f for name, f in locals().items() if name.startswith("t_")}
    for name, h in (
        ("s", 0), ("z2", 0), ("x", 0), ("zz", 0), ("x", 1), ("fx", 0), ("z2", 1), ("f2", 0), ("fz", 0),
        ("norm", 0), ("px", 0), ("qz", 0), ("qx", 0), ("q2", 0), ("fx", 1), ("f3", 0), ("p3", 0), ("zz", 1),
        ("f4", 0), ("p0", 0), ("q3", 0), ("p4", 0), ("q4", 0), ("pz", 0), ("p2", 0), ("f2", 1), ("att", 0),
        ("s", 1), ("px", 1), ("opa", 0), ("opb", 0), ("p2", 1), ("f3", 1), ("f4", 1), ("p4", 1), ("q2", 1),
        ("p0", 1), ("fz", 1), ("pz", 1), ("r1", 0), ("r1b", 0), ("q3", 1), ("qx", 1), ("qz", 1), ("q4", 1),
        ("p3", 1), ("att", 1), ("opa", 1), ("r3", 0), ("opb", 1), ("nb", 0),
    ):
        tasks[name](h)
    loads[8].wait()
    loads[9].wait()
    up_product(0)
    t_r1(1)
    t_r1b(1)

    @pl.loop(0, N_K + 7)
    def _(step):
        pl.when(step == 2)(lambda: t_r3(1))
        pl.when(step == 4)(lambda: t_nb(1))
        for f, lag in (
            (pair_sum, 0), (up_product, -1), (second_sum, 1), (third_sum, 2), (down_product, 7),
            (activate, 3), (to_sibling, 6), (spread, 4), (spread_across, 5),
        ):
            k = step - lag
            pl.when(jnp.logical_and(k >= 0, k < N_K))(lambda f=f, k=k: f(k))

    for h in range(2):
        total = resid[h].astype(F32) + down[CHUNK_OF[h, 0]].astype(F32)
        for r in (1, 2, 3, 4):
            fin_arrived(h, r)
            total += fin[h, r].astype(F32)
        o_ref[h] = total.astype(BF16)

    others_a.wait_send()
    for h in range(2):
        others_f[h].wait_send()
        all_of(nb.at[h, pl.ds(0, 7)], nb_send.at[h], nb_recv.at[0, 0]).wait_send()
    all_of(tok.at[pl.ds(0, 15)], ag_send.at[0], ag_recv.at[0, 0]).wait_send()
    all_of(part.at[oc], sib_send.at[0], sib_recv.at[0, 0]).wait_send()
    all_of(part.at[c, pl.ds(0, 7)], red_send.at[0], red_recv.at[0, 0]).wait_send()
    all_of(down.at[pl.ds(0, 14)], dp_send.at[0], dp_recv.at[0, 0]).wait_send()
    all_of(act.at[pl.ds(0, BLOCKS)], act_send.at[0], recv.at[0, 0]).wait_send()

    @pl.loop(N_K - RING, N_K)
    def _(k):
        sums_sent(k)


def per_device(
    tokens, segment_ids, gain_attn, w_query, w_key, w_value, w_output, gain_ffn, w_up, w_down
):
    rows, share = tokens.shape
    vmem, hbm = pl.BlockSpec(memory_space=pltpu.VMEM), pl.BlockSpec(memory_space=pl.ANY)
    half = (HALF, share)
    dma = pltpu.SemaphoreType.DMA

    def b(*shape):
        return pltpu.VMEM(shape, BF16)

    def f(*shape):
        return pltpu.VMEM(shape, F32)

    out = pl.pallas_call(
        kernel,
        out_shape=jax.ShapeDtypeStruct((2, *half), BF16),
        in_specs=[hbm] * 10,
        out_specs=vmem,
        scratch_shapes=[
            pltpu.VMEM(segment_ids.shape, jnp.int32), f(N_G, 1, share), f(1, share),
            b(*w_query.shape), b(*w_query.shape), b(*w_query.shape), b(*w_output.shape),
            b(*w_up.shape), b(4, 512, share),
            b(N_G, 2, *half), f(2, HALF, 768), b(2, HALF, 256), b(2, 8, 2, *half), b(8, 2, *half),
            b(7, 2, *half), f(2, 8, HALF), f(2, 8, HALF), f(N_G, 2, 8, HALF), f(2, N_G, 8, HALF),
            f(2, *half), f(2, *half), b(2, *half),
            b(2, N_DP, *half), b(RING, 2, 8, 2, 16, 512), b(N_K, 8, 2, 16, 512), b(N_K, 7, 2, 16, 512),
            b(N_K, 2, 8, 2, 16, 512), f(*half), b(N_K, *half), b(2, N_DP, *half),
            dma((10,)), dma((1,)), dma((N_G, 2)), dma((1,)), dma((8, 2)), dma((1,)), dma((7, 2)),
            dma((1,)), dma((1,)), dma((2,)), dma((2,)),
            dma((RING,)), dma((1,)), dma((RING, len(GROUPS))), dma((2,)), dma((2, N_DP)), dma((1,)), dma((2, N_DP)),
        ],
        compiler_params=pltpu.CompilerParams(
            collective_id=0, has_side_effects=True, vmem_limit_bytes=62 << 20
        ),
        name="layer",
    )(
        tokens.reshape(2, *half), segment_ids, gain_attn.reshape(N_G, 1, share),
        gain_ffn.reshape(N_G, 1, share), w_query, w_key, w_value, w_output, w_up,
        w_down.reshape(4, 512, share),
    )
    return out.reshape(rows, share)


def solution(mesh):
    return jax.shard_map(
        per_device,
        mesh=mesh,
        in_specs=(
            P("dp", ("section", "tensor")),
            P("dp", None),
            P(),
            P(None, ("section", "tensor")),
            P(None, ("section", "tensor")),
            P(None, ("section", "tensor")),
            P(("section", "tensor"), None),
            P(),
            P(("section", "tensor"), "dp"),
            P("dp", ("section", "tensor")),
        ),
        out_specs=P("dp", ("section", "tensor")),
        check_vma=False,
    )
```

```python
import jax
import jax.numpy as jnp
from jax import lax
from jax.experimental import pallas as pl
from jax.experimental.pallas import tpu as pltpu
from jax.sharding import PartitionSpec as P

MESH = pl.DeviceIdType.MESH
HD = 128
F32 = jnp.float32
BF16 = jnp.bfloat16
N_G = 16
N_DP = 8
HALF = 128
WIDE = 512

CHUNKS = (
    (0, 0), (0, 3), (0, 1), (0, 2), (0, 7), (0, 5), (1, 3), (1, 1),
    (0, 6), (1, 7), (1, 6), (1, 5), (0, 4), (1, 2), (1, 4), (1, 0),
)
N_K = len(CHUNKS)
CHUNK_OF = {chunk: k for k, chunk in enumerate(CHUNKS)}
FORWARD_AT = (2, 7)
DIRECT_SUM = (0, 4)
DIRECT_GATHER = 11
RING = 8

(
    SB, RX1, RZP, RZM, FX, FZP1, FZM0, H0, H1, FZP0, FZM1, FZP, FZM, FZ2,
    AX, AZP, AZM, XZP, XZM, XZ2, AS, ZH0, ZH1, AZ2,
) = range(24)
GROUPS = (
    (SB,), (RX1,), (RZP, RZM), (FX, FZP1, FZM0, FZP0, FZM1, FZP, FZM, FZ2), (H0,), (H1,),
    (AX,), (AZP,), (AZM,), (XZP, XZM, XZ2), (AS,), (ZH0, ZH1, AZ2),
)
GROUP_OF = {kind: n for n, group in enumerate(GROUPS) for kind in group}
L_RX1, L_RZP, L_RZM, L_FX, L_FZP, L_FZM, L_H = range(7)
BLOCKS = 15


def remote(src, dst, send_sem, recv_sem, device):
    return pltpu.make_async_remote_copy(
        src_ref=src,
        dst_ref=dst,
        send_sem=send_sem,
        recv_sem=recv_sem,
        device_id=device,
        device_id_type=MESH,
    )


def pick(k, values):
    result = jnp.int32(values[0])
    for i, value in enumerate(values[1:], 1):
        result = jnp.where(k == i, jnp.int32(value), result)
    return result


def rows_to_columns(row, width):
    column = jnp.transpose(jnp.broadcast_to(row, (128, row.shape[1])))
    return jnp.concatenate([column] * (width // 128), axis=1)


def partial_stats(values):
    ones = jnp.ones((8, values.shape[1]), BF16)
    dims = (((1,), (1,)), ((), ()))
    wide = values.astype(F32)
    square = wide * wide
    high = square.astype(BF16)
    low = (square - high.astype(F32)).astype(BF16)
    total = lax.dot_general(ones, values, dims, preferred_element_type=F32)
    second = lax.dot_general(ones, high, dims, preferred_element_type=F32)
    second += lax.dot_general(ones, low, dims, preferred_element_type=F32)
    return jnp.where(lax.broadcasted_iota(jnp.int32, total.shape, 0) == 0, total, second)


def kernel(
    tok_hbm, seg_hbm, gain_a_hbm, gain_f_hbm, wq_hbm, wk_hbm, wv_hbm, wo_hbm, wu_hbm, wd_hbm,
    o_ref,
    seg, gain_a, gain_f, wq, wk, wv, wo, wu, wd,
    tok, acc, ctx, part, sib, red, own_a, own_f, stats_a, stats_f, mu, scale, resid,
    nb, up, sb, land, act, part_down, down, fin,
    w_sem, ag_send, ag_recv, sib_send, sib_recv, red_send, red_recv, sa_send, sa_recv, sf_send, sf_recv,
    sum_send, act_send, recv, nb_send, nb_recv, dp_send, dp_recv,
):
    a = lax.axis_index("section")
    t = lax.axis_index("tensor")
    d = lax.axis_index("dp")
    z, c = t // 2, t % 2
    xh, y = d // 4, d % 4
    oa, oc = 1 - a, 1 - c
    zp, zm, z2 = (z + 1) % 4, (z + 3) % 4, (z + 2) % 4
    me = a * 8 + t

    def dev(a_, z_, c_):
        return {"section": a_, "tensor": z_ * 2 + c_}

    def slot(a_, z_, c_):
        return a_ * 8 + z_ * 2 + c_

    def at_dp(d_):
        return {"dp": d_}

    def y_of(dy):
        return xh * 4 + (y + dy) % 4

    def peer(r):
        i = (me + r) % N_G
        return i, {"section": i // 8, "tensor": i % 8}

    D_X, D_ZP, D_ZM = dev(oa, z, c), dev(a, zp, c), dev(a, zm, c)
    D_Z2, D_S = dev(a, z2, c), dev(a, z, oc)
    across = (1 - xh) * 4 + y
    dp_peers = [at_dp(y_of(dy)) for dy in (1, 2, 3)] + [at_dp(across)]

    barrier = pltpu.get_barrier_semaphore()

    @pl.loop(1, N_G)
    def _(r):
        pl.semaphore_signal(barrier, inc=1, device_id=peer(r)[1], device_id_type=MESH)

    for device in dp_peers:
        pl.semaphore_signal(barrier, inc=1, device_id=device, device_id_type=MESH)

    pairs = (
        (tok_hbm, tok.at[me]), (gain_a_hbm, gain_a), (seg_hbm, seg), (gain_f_hbm.at[me], gain_f),
        (wq_hbm, wq), (wk_hbm, wk), (wv_hbm, wv), (wo_hbm, wo), (wu_hbm, wu), (wd_hbm, wd),
    )
    loads = [pltpu.make_async_copy(h, v, w_sem.at[n]) for n, (h, v) in enumerate(pairs)]
    for load in loads:
        load.start()
    loads[0].wait()
    for h in range(2):
        own_a[h] = partial_stats(tok[me, h])
    stats_a[0] = own_a[...]
    pl.semaphore_wait(barrier, N_G - 1 + len(dp_peers))

    def stat_a(r):
        i, device = peer(r)
        return remote(own_a, stats_a.at[r], sa_send.at[0], sa_recv.at[0], device)

    def stat_f(h, r):
        i, device = peer(r)
        return remote(own_f.at[h], stats_f.at[h, r], sf_send.at[h], sf_recv.at[h], device)

    def all_of(ref, send_sem, recv_sem):
        return remote(ref, ref, send_sem, recv_sem, D_X)

    others_a = all_of(stats_a.at[pl.ds(1, N_G - 1)], sa_send.at[0], sa_recv.at[0])
    others_f = [all_of(stats_f.at[h, pl.ds(1, N_G - 1)], sf_send.at[h], sf_recv.at[h]) for h in range(2)]

    def norm_from(total, h):
        mean = total[0:1] / 8192.0
        second = total[1:2] / 8192.0
        inverse = lax.rsqrt(second - mean * mean + 1e-05)
        mu[h] = rows_to_columns(mean, WIDE)
        scale[h] = rows_to_columns(inverse, WIDE)

    def ag(s, h, device):
        remote(tok.at[s, h], tok.at[s, h], ag_send.at[0], ag_recv.at[s, h], device).start()

    def arrived(s, h):
        remote(tok.at[s, h], tok.at[s, h], ag_send.at[0], ag_recv.at[s, h], D_X).wait_recv()

    s_own, s_x, s_zp, s_zm = slot(a, z, c), slot(oa, z, c), slot(a, zp, c), slot(a, zm, c)
    s_z2, s_xzp, s_xzm, s_xz2 = slot(a, z2, c), slot(oa, zp, c), slot(oa, zm, c), slot(oa, z2, c)

    def other(s):
        return s + oc - c

    def project(s, h):
        x = (tok[s, h].astype(F32) - mu[h]) * scale[h] * gain_a[s]
        x = x.astype(BF16)
        at = pl.ds(pl.multiple_of(s * WIDE, WIDE), WIDE)
        for n, w in enumerate((wq, wk, wv)):
            acc[h, :, n * 256 : (n + 1) * 256] += jnp.dot(x, w[at, :], preferred_element_type=F32)

    def t_x(h):
        ag(s_own, h, D_X)

    def t_zz(h):
        ag(s_own, h, D_ZP)
        ag(s_own, h, D_ZM)

    def t_s(h):
        ag(s_own, h, D_S)

    def t_z2(h):
        ag(s_own, h, D_Z2)

    def t_fx(h):
        arrived(s_x, h)
        ag(s_x, h, D_ZP)
        ag(s_x, h, D_ZM)
        ag(s_x, h, D_S)

    def t_fz(h):
        for s in (s_zp, s_zm):
            arrived(s, h)
            ag(s, h, D_S)

    def t_f2(h):
        arrived(s_z2, h)
        ag(s_z2, h, D_X)
        ag(s_z2, h, D_S)

    def t_f3(h):
        for s in (s_xzp, s_xzm):
            arrived(s, h)
            ag(s, h, D_S)

    def t_f4(h):
        arrived(s_xz2, h)
        ag(s_xz2, h, D_S)

    def t_stat(h):
        @pl.loop(1, N_G)
        def _(r):
            stat_a(r).start()

    def t_norm(h):
        if h == 0:

            others_a.wait_recv()
            for n in range(2):
                norm_from(jnp.sum(stats_a[:, n], axis=0), n)
            acc[...] = jnp.zeros_like(acc)
            for n in (1, 2, 3, 4, 5, 6):
                loads[n].wait()

    def t_p0(h):
        project(s_own, h)
        arrived(other(s_own), h)
        project(other(s_own), h)

    def t_px(h):
        project(s_x, h)

    def t_pz(h):
        project(s_zp, h)
        project(s_zm, h)

    def t_p2(h):
        project(s_z2, h)

    def t_p3(h):
        project(s_xzp, h)
        project(s_xzm, h)

    def t_p4(h):
        project(s_xz2, h)

    def others(h, *slots):
        for s in slots:
            arrived(other(s), h)
            project(other(s), h)

    def t_qx(h):
        others(h, s_x)

    def t_qz(h):
        others(h, s_zp, s_zm)

    def t_q2(h):
        others(h, s_z2)

    def t_q3(h):
        others(h, s_xzp, s_xzm)

    def t_q4(h):
        others(h, s_xz2)

    def t_att(h):
        keys = (h + 1) * HALF
        seg_row = seg[...].astype(F32)
        seg_col = rows_to_columns(seg_row[:, h * HALF : (h + 1) * HALF], keys)
        at_q = lax.broadcasted_iota(jnp.int32, (HALF, keys), 0) + h * HALF
        at_k = lax.broadcasted_iota(jnp.int32, (HALF, keys), 1)
        keep = jnp.logical_and(at_q >= at_k, seg_col == seg_row[:, :keys])
        for head in range(2):

            def part_of(n, halves):
                cols = slice(n * 256 + head * HD, n * 256 + (head + 1) * HD)
                return jnp.concatenate([acc[i, :, cols].astype(BF16) for i in halves], axis=0)

            q, k, v = part_of(0, (h,)), part_of(1, range(h + 1)), part_of(2, range(h + 1))
            scores = lax.dot_general(q, k, (((1,), (1,)), ((), ())), preferred_element_type=F32)
            scores = jnp.where(keep, scores * HD ** (-0.5), -1e30)
            expo = jnp.exp(scores - jnp.max(scores, axis=-1, keepdims=True))
            probs = (expo / jnp.sum(expo, axis=-1, keepdims=True)).astype(BF16)
            context = jnp.dot(probs, v, preferred_element_type=F32)
            ctx[h, :, head * HD : (head + 1) * HD] = context.astype(BF16)

    order = ((oa, z2), (oa, zp), (oa, zm), (a, zp), (a, zm), (a, z2), (oa, z), (a, z))

    def term(s, h):
        at = pl.ds(pl.multiple_of(s * WIDE, WIDE), WIDE)
        return jnp.dot(ctx[h], wo[:, at], preferred_element_type=F32)

    def sib_copy(n, h):
        return remote(part.at[oc, n, h], sib.at[n, h], sib_send.at[0], sib_recv.at[n, h], D_S)

    def t_opa(h):
        if h == 0:
            loads[7].wait()
        for n, (a_, z_) in enumerate(order):
            part[oc, n, h] = term(slot(a_, z_, oc), h).astype(BF16)
            sib_copy(n, h).start()

    red_to = (D_X, D_ZP, D_ZM, D_ZP, D_ZM, D_Z2, D_X)

    def red_copy(n, h):
        return remote(part.at[c, n, h], red.at[n, h], red_send.at[0], red_recv.at[n, h], red_to[n])

    def t_opb(h):
        for n, (a_, z_) in enumerate(order):
            mine = term(slot(a_, z_, c), h)
            sib_copy(n, h).wait_recv()
            part[c, n, h] = (mine + sib[n, h].astype(F32)).astype(BF16)
            if n < 5:
                red_copy(n, h).start()

    def add_landed(n, h, *landings):
        total = part[c, n, h].astype(F32)
        for i in landings:
            red_copy(i, h).wait_recv()
            total += red[i, h].astype(F32)
        return total

    def t_r1(h):
        part[c, 5, h] = add_landed(5, h, 0).astype(BF16)
        red_copy(5, h).start()

    def t_r1b(h):
        part[c, 6, h] = add_landed(6, h, 1, 2).astype(BF16)
        red_copy(6, h).start()

    def t_r3(h):
        total = tok[me, h].astype(F32) + add_landed(7, h, 3, 4, 6, 5)
        resid[h] = total.astype(BF16)
        own_f[h] = partial_stats(resid[h])
        stats_f[h, 0] = own_f[h]

        @pl.loop(1, N_G)
        def _(r):
            stat_f(h, r).start()

    def nb_copy(h, s, device):
        return remote(nb.at[h, s], nb.at[h, s], nb_send.at[h], nb_recv.at[h, s], device)

    def nb_sends(h):
        to = (across, y_of(1), y_of(3), y_of(2))
        return [nb_copy(h, d, at_dp(d_)) for d_ in to]

    def nb_forwards(h):
        return [nb_copy(h, across, at_dp(y_of(dy))) for dy in (1, 3, 2)]

    def nb_arrived(h, s):
        nb_copy(h, s, at_dp(across)).wait_recv()

    def t_nb(h):
        others_f[h].wait_recv()
        norm_from(jnp.sum(stats_f[h], axis=0), h)
        normed = (resid[h].astype(F32) - mu[h]) * scale[h] * gain_f[...]
        nb[h, d] = normed.astype(BF16)
        for copy in nb_sends(h):
            copy.start()

    def half_of(k):
        return pick(k, [h for h, r in CHUNKS])

    def replica_of(k):
        return pick(k, [r for h, r in CHUNKS])

    def block(k, a_, z_):
        return up.at[k % RING, c, a_ * 4 + z_]

    def act_block(k, a_, z_):
        return act.at[k, c, a_ * 4 + z_]

    def copy_of(kind, k):
        at = land.at[k]
        src, dst, device = {
            SB: lambda: (up.at[k % RING, oc], sb.at[k], D_S),
            RX1: lambda: (block(k, oa, z2), at.at[L_RX1], D_X),
            RZP: lambda: (block(k, oa, zp), at.at[L_RZP], D_ZP),
            RZM: lambda: (block(k, oa, zm), at.at[L_RZM], D_ZM),
            FX: lambda: (block(k, oa, z), at.at[L_FX], D_X),
            FZP1: lambda: (block(k, a, zp).at[1], at.at[L_FZP, 1], D_ZP),
            FZM0: lambda: (block(k, a, zm).at[0], at.at[L_FZM, 0], D_ZM),
            H0: lambda: (block(k, a, z2).at[0], at.at[L_H, 0], D_ZP),
            H1: lambda: (block(k, a, z2).at[1], at.at[L_H, 1], D_ZM),
            FZP0: lambda: (block(k, a, zp).at[0], at.at[L_FZP, 0], D_ZP),
            FZM1: lambda: (block(k, a, zm).at[1], at.at[L_FZM, 1], D_ZM),
            FZP: lambda: (block(k, a, zp), at.at[L_FZP], D_ZP),
            FZM: lambda: (block(k, a, zm), at.at[L_FZM], D_ZM),
            FZ2: lambda: (block(k, a, z2), at.at[L_H], D_Z2),
            AX: lambda: (act_block(k, a, z),) * 2 + (D_X,),
            AZP: lambda: (act_block(k, a, z),) * 2 + (D_ZP,),
            AZM: lambda: (act_block(k, a, z),) * 2 + (D_ZM,),
            AZ2: lambda: (act_block(k, a, z),) * 2 + (D_Z2,),
            XZP: lambda: (act_block(k, oa, z),) * 2 + (D_ZP,),
            XZM: lambda: (act_block(k, oa, z),) * 2 + (D_ZM,),
            XZ2: lambda: (act_block(k, a, z2),) * 2 + (D_X,),
            ZH0: lambda: (act_block(k, a, zm).at[0],) * 2 + (D_ZP,),
            ZH1: lambda: (act_block(k, a, zp).at[1],) * 2 + (D_ZM,),
            AS: lambda: (act.at[k, c],) * 2 + (D_S,),
        }[kind]()
        sent = sum_send.at[k % RING] if kind < AX else act_send.at[0]
        return remote(src, dst, sent, recv.at[k % RING, GROUP_OF[kind]], device)

    def got(k, kind, ref):
        all_of(ref, act_send.at[0], recv.at[k % RING, GROUP_OF[kind]]).wait_recv()

    def give(k, *kinds):
        for kind in kinds:
            copy_of(kind, k).start()

    def either(condition, yes, no):
        pl.when(condition)(yes)
        pl.when(jnp.logical_not(condition))(no)

    def sums_sent(k):
        i = k % RING
        all_of(act.at[pl.ds(0, BLOCKS), 0, 0], sum_send.at[i], recv.at[0, 0]).wait_send()

    def sums_direct(k):
        return jnp.logical_and(k >= DIRECT_SUM[0], k < DIRECT_SUM[1])

    def up_product(k):
        h, r = half_of(k), replica_of(k)
        s = ((xh + r // 4) % 2) * 4 + (y + r % 4) % 4
        for n in range(2):

            @pl.when(k == FORWARD_AT[n])
            def _():
                nb_arrived(n, across)
                for copy in nb_forwards(n):
                    copy.start()

        @pl.when(pick(k, [int(r_ not in (0, 4)) for _, r_ in CHUNKS]) == 1)
        def _():
            nb_arrived(h, s)

        @pl.when(k >= RING)
        def _():
            sums_sent(k - RING)

        x = nb[h, s]
        for n in range(4):
            r_ = jnp.dot(x, wu[:, n * 512 : (n + 1) * 512], preferred_element_type=F32)
            up[k % RING, n // 2, :, n % 2] = r_.astype(BF16).reshape(8, 16, 512)
        give(k, SB)

    def pair_sum(k):
        got(k, SB, sb.at[k])
        i = k % RING
        up[i, c] = (up[i, c].astype(F32) + sb[k].astype(F32)).astype(BF16)
        give(k, RX1, RZP, RZM)
        either(sums_direct(k), lambda: give(k, FZP, FZM), lambda: give(k, FZP1, FZM0))

    def second_sum(k):
        i = k % RING
        got(k, RX1, land.at[k, L_RX1])
        b = a * 4 + z2
        up[i, c, b] = (up[i, c, b].astype(F32) + land[k, L_RX1].astype(F32)).astype(BF16)
        either(sums_direct(k), lambda: give(k, FZ2), lambda: give(k, H0, H1))
        got(k, RZP, land.at[k, pl.ds(L_RZP, 2)])
        b = oa * 4 + z
        both = land[k, L_RZP].astype(F32) + land[k, L_RZM].astype(F32)
        up[i, c, b] = (up[i, c, b].astype(F32) + both).astype(BF16)
        give(k, FX)

    def third_sum(k):
        i = k % RING

        @pl.when(jnp.logical_not(sums_direct(k)))
        def _():
            for kind, then, z_, half in ((H0, FZP0, zp, 0), (H1, FZM1, zm, 1)):
                got(k, kind, land.at[k, L_H, half])
                b = a * 4 + z_
                both = up[i, c, b, half].astype(F32) + land[k, L_H, half].astype(F32)
                up[i, c, b, half] = both.astype(BF16)
                give(k, then)

    def activate(k):
        i, b = k % RING, a * 4 + z

        def finish(pre, *landings):
            for n in landings:
                pre += land[k, n].astype(F32)
            inner = 0.7978845608028654 * (pre + 0.044715 * (pre * pre * pre))
            act[k, c, b] = (0.5 * pre * (1.0 + jnp.tanh(inner))).astype(BF16)

        def from_four():
            got(k, FX, land.at[k, pl.ds(L_FX, 4)])
            finish(up[i, c, b].astype(F32), L_FZP, L_FZM, L_FX, L_H)

        def from_three():
            got(k, FX, land.at[k, pl.ds(L_FX, 3)])
            finish(up[i, c, b].astype(F32), L_FZP, L_FZM, L_FX)

        either(sums_direct(k), from_four, from_three)

        @pl.when(k >= DIRECT_GATHER)
        def _():
            give(k, AZ2)

        give(k, AX, AZP, AZM)

    def spread(k):
        got(k, AX, act_block(k, oa, z))
        give(k, XZP, XZM)

        def direct():
            got(k, AZ2, act_block(k, a, z2))
            give(k, XZ2)

        def halves():
            got(k, AZP, act_block(k, a, zm))
            give(k, ZH0)
            got(k, AZM, act_block(k, a, zp))
            give(k, ZH1)

        either(k >= DIRECT_GATHER, direct, halves)

    def spread_across(k):
        def halves():
            got(k, ZH0, act_block(k, a, z2))
            give(k, XZ2)

        def direct():
            got(k, AZP, act_block(k, a, zm))
            got(k, AZM, act_block(k, a, zp))

        either(k >= DIRECT_GATHER, direct, halves)

    def down_half(k, c_):
        r = jnp.zeros((HALF, WIDE), F32)
        for q in range(2):
            x = act[k, c_, :, q].reshape(HALF, 512)
            r += jnp.dot(x, wd[c_ * 2 + q], preferred_element_type=F32)
        return r

    def to_sibling(k):
        got(k, XZP, act.at[k, c, pl.ds(0, 3)])
        give(k, AS)
        part_down[...] = down_half(k, c)

    def dp_copy(k):
        r = replica_of(k)
        x_ = (xh + pick(k, [int(r_ == 4) for _, r_ in CHUNKS])) % 2
        to = at_dp(x_ * 4 + (y + r % 4) % 4)
        return remote(down.at[k], fin.at[half_of(k), r], dp_send.at[0], dp_recv.at[half_of(k), r], to)

    def fin_arrived(h, r):
        remote(down.at[0], fin.at[h, r], dp_send.at[0], dp_recv.at[h, r], at_dp(across)).wait_recv()

    def is_sent(k):
        return pick(k, [int(r_ != 0) for _, r_ in CHUNKS]) == 1

    def down_product(k):
        got(k, AS, act.at[k, oc])
        down[k] = (part_down[...] + down_half(k, oc)).astype(BF16)
        for h in range(2):

            @pl.when(k == CHUNK_OF[h, 4])
            def _():
                total = down[k].astype(F32)
                for r in (5, 6, 7):
                    fin_arrived(h, r)
                    total += fin[h, r].astype(F32)
                down[k] = total.astype(BF16)

        @pl.when(is_sent(k))
        def _():
            dp_copy(k).start()

    tasks = {name[2:]: f for name, f in locals().items() if name.startswith("t_")}
    for name, h in (
        ("z2", 0), ("x", 0), ("stat", 0), ("s", 0), ("zz", 0), ("x", 1), ("fx", 0), ("fz", 0), ("f2", 0), ("zz", 1),
        ("norm", 0), ("p0", 0), ("pz", 0), ("fx", 1), ("px", 1), ("f3", 0), ("p2", 0), ("qz", 0), ("q2", 0),
        ("p3", 0), ("px", 0), ("qx", 1), ("f4", 0), ("p4", 0), ("q3", 0), ("z2", 1), ("qx", 0), ("fz", 1),
        ("q4", 0), ("att", 0), ("opa", 0), ("s", 1), ("opb", 0), ("p0", 1), ("f2", 1), ("r1b", 0), ("r1", 0),
        ("qz", 1), ("f3", 1), ("pz", 1), ("f4", 1), ("p3", 1), ("q2", 1), ("q3", 1), ("p2", 1), ("p4", 1),
        ("q4", 1), ("att", 1), ("r3", 0), ("opa", 1), ("opb", 1), ("nb", 0),
    ):
        tasks[name](h)
    loads[8].wait()
    loads[9].wait()
    up_product(0)
    t_r1b(1)
    t_r1(1)

    @pl.loop(0, N_K + 7)
    def _(step):
        pl.when(step == 2)(lambda: t_r3(1))
        pl.when(step == 4)(lambda: t_nb(1))
        for f, lag in (
            (pair_sum, 0), (up_product, -1), (second_sum, 1), (third_sum, 2), (activate, 3),
            (down_product, 7), (to_sibling, 6), (spread, 4), (spread_across, 5),
        ):
            k = step - lag
            pl.when(jnp.logical_and(k >= 0, k < N_K))(lambda f=f, k=k: f(k))

    for h in range(2):
        total = resid[h].astype(F32) + down[CHUNK_OF[h, 0]].astype(F32)
        for r in (1, 2, 3, 4):
            fin_arrived(h, r)
            total += fin[h, r].astype(F32)
        o_ref[h] = total.astype(BF16)

    others_a.wait_send()
    for h in range(2):
        others_f[h].wait_send()
        all_of(nb.at[h, pl.ds(0, 7)], nb_send.at[h], nb_recv.at[0, 0]).wait_send()
    all_of(tok.at[pl.ds(0, 15)], ag_send.at[0], ag_recv.at[0, 0]).wait_send()
    all_of(part.at[oc], sib_send.at[0], sib_recv.at[0, 0]).wait_send()
    all_of(part.at[c, pl.ds(0, 7)], red_send.at[0], red_recv.at[0, 0]).wait_send()
    all_of(down.at[pl.ds(0, 14)], dp_send.at[0], dp_recv.at[0, 0]).wait_send()
    all_of(act.at[pl.ds(0, BLOCKS)], act_send.at[0], recv.at[0, 0]).wait_send()

    @pl.loop(N_K - RING, N_K)
    def _(k):
        sums_sent(k)


def per_device(
    tokens, segment_ids, gain_attn, w_query, w_key, w_value, w_output, gain_ffn, w_up, w_down
):
    rows, share = tokens.shape
    vmem, hbm = pl.BlockSpec(memory_space=pltpu.VMEM), pl.BlockSpec(memory_space=pl.ANY)
    half = (HALF, share)
    dma = pltpu.SemaphoreType.DMA

    def b(*shape):
        return pltpu.VMEM(shape, BF16)

    def f(*shape):
        return pltpu.VMEM(shape, F32)

    out = pl.pallas_call(
        kernel,
        out_shape=jax.ShapeDtypeStruct((2, *half), BF16),
        in_specs=[hbm] * 10,
        out_specs=vmem,
        scratch_shapes=[
            pltpu.VMEM(segment_ids.shape, jnp.int32), f(N_G, 1, share), f(1, share),
            b(*w_query.shape), b(*w_query.shape), b(*w_query.shape), b(*w_output.shape),
            b(*w_up.shape), b(4, 512, share),
            b(N_G, 2, *half), f(2, HALF, 768), b(2, HALF, 256), b(2, 8, 2, *half), b(8, 2, *half),
            b(7, 2, *half), f(2, 8, HALF), f(2, 8, HALF), f(N_G, 2, 8, HALF), f(2, N_G, 8, HALF),
            f(2, *half), f(2, *half), b(2, *half),
            b(2, N_DP, *half), b(RING, 2, 8, 2, 16, 512), b(N_K, 8, 2, 16, 512), b(N_K, 7, 2, 16, 512),
            b(N_K, 2, 8, 2, 16, 512), f(*half), b(N_K, *half), b(2, N_DP, *half),
            dma((10,)), dma((1,)), dma((N_G, 2)), dma((1,)), dma((8, 2)), dma((1,)), dma((7, 2)),
            dma((1,)), dma((1,)), dma((2,)), dma((2,)),
            dma((RING,)), dma((1,)), dma((RING, len(GROUPS))), dma((2,)), dma((2, N_DP)), dma((1,)), dma((2, N_DP)),
        ],
        compiler_params=pltpu.CompilerParams(
            collective_id=0, has_side_effects=True, vmem_limit_bytes=62 << 20
        ),
        name="layer",
    )(
        tokens.reshape(2, *half), segment_ids, gain_attn.reshape(N_G, 1, share),
        gain_ffn.reshape(N_G, 1, share), w_query, w_key, w_value, w_output, w_up,
        w_down.reshape(4, 512, share),
    )
    return out.reshape(rows, share)


def solution(mesh):
    return jax.shard_map(
        per_device,
        mesh=mesh,
        in_specs=(
            P("dp", ("section", "tensor")),
            P("dp", None),
            P(),
            P(None, ("section", "tensor")),
            P(None, ("section", "tensor")),
            P(None, ("section", "tensor")),
            P(("section", "tensor"), None),
            P(),
            P(("section", "tensor"), "dp"),
            P("dp", ("section", "tensor")),
        ),
        out_specs=P("dp", ("section", "tensor")),
        check_vma=False,
    )
```

```python
import jax
import jax.numpy as jnp
from jax import lax
from jax.experimental import pallas as pl
from jax.experimental.pallas import tpu as pltpu
from jax.sharding import PartitionSpec as P

MESH = pl.DeviceIdType.MESH
HD = 128
F32 = jnp.float32
BF16 = jnp.bfloat16
N_G = 16
N_DP = 8
HALF = 128
WIDE = 512

CHUNKS = (
    (0, 0), (0, 3), (0, 1), (0, 2), (0, 7), (0, 5), (1, 3), (1, 1),
    (0, 6), (1, 7), (1, 6), (1, 5), (0, 4), (1, 2), (1, 4), (1, 0),
)
N_K = len(CHUNKS)
CHUNK_OF = {chunk: k for k, chunk in enumerate(CHUNKS)}
FORWARD_AT = (2, 7)
DIRECT_SUM = (0, 4)
DIRECT_GATHER = 11
RING = 8
AHEAD = 3

(
    SB, RX1, RZP, RZM, FX, FZP1, FZM0, H0, H1, FZP0, FZM1, FZP, FZM, FZ2,
    AX, AZP, AZM, XZP, XZM, XZ2, AS, ZH0, ZH1, AZ2,
) = range(24)
GROUPS = (
    (SB,), (RX1,), (RZP, RZM), (FX, FZP1, FZM0, FZP0, FZM1, FZP, FZM, FZ2), (H0,), (H1,),
    (AX,), (AZP,), (AZM,), (XZP, XZM, XZ2), (AS,), (ZH0, ZH1, AZ2),
)
GROUP_OF = {kind: n for n, group in enumerate(GROUPS) for kind in group}
L_RX1, L_RZP, L_RZM, L_FX, L_FZP, L_FZM, L_H = range(7)
BLOCKS = 15


def remote(src, dst, send_sem, recv_sem, device):
    return pltpu.make_async_remote_copy(
        src_ref=src,
        dst_ref=dst,
        send_sem=send_sem,
        recv_sem=recv_sem,
        device_id=device,
        device_id_type=MESH,
    )


def pick(k, values):
    result = jnp.int32(values[0])
    for i, value in enumerate(values[1:], 1):
        result = jnp.where(k == i, jnp.int32(value), result)
    return result


def rows_to_columns(row, width):
    column = jnp.transpose(jnp.broadcast_to(row, (128, row.shape[1])))
    return jnp.concatenate([column] * (width // 128), axis=1)


def partial_stats(values):
    ones = jnp.ones((8, values.shape[1]), BF16)
    dims = (((1,), (1,)), ((), ()))
    wide = values.astype(F32)
    square = wide * wide
    high = square.astype(BF16)
    low = (square - high.astype(F32)).astype(BF16)
    total = lax.dot_general(ones, values, dims, preferred_element_type=F32)
    second = lax.dot_general(ones, high, dims, preferred_element_type=F32)
    second += lax.dot_general(ones, low, dims, preferred_element_type=F32)
    return jnp.where(lax.broadcasted_iota(jnp.int32, total.shape, 0) == 0, total, second)


def kernel(
    tok_hbm, seg_hbm, gain_a_hbm, gain_f_hbm, wq_hbm, wk_hbm, wv_hbm, wo_hbm, wu_hbm, wd_hbm,
    o_ref,
    seg, gain_a, gain_f, wq, wk, wv, wo, wu, wd,
    tok, acc, ctx, part, sib, red, own_a, own_f, stats_a, stats_f, mu, scale, resid,
    nb, up, sb, land, act, part_down, down, fin,
    w_sem, ag_send, ag_recv, sib_send, sib_recv, red_send, red_recv, sa_send, sa_recv, sf_send, sf_recv,
    sum_send, act_send, recv, nb_send, nb_recv, dp_send, dp_recv,
):
    a = lax.axis_index("section")
    t = lax.axis_index("tensor")
    d = lax.axis_index("dp")
    z, c = t // 2, t % 2
    xh, y = d // 4, d % 4
    oa, oc = 1 - a, 1 - c
    zp, zm, z2 = (z + 1) % 4, (z + 3) % 4, (z + 2) % 4
    me = a * 8 + t

    def dev(a_, z_, c_):
        return {"section": a_, "tensor": z_ * 2 + c_}

    def slot(a_, z_, c_):
        return a_ * 8 + z_ * 2 + c_

    def at_dp(d_):
        return {"dp": d_}

    def y_of(dy):
        return xh * 4 + (y + dy) % 4

    def peer(r):
        i = (me + r) % N_G
        return i, {"section": i // 8, "tensor": i % 8}

    D_X, D_ZP, D_ZM = dev(oa, z, c), dev(a, zp, c), dev(a, zm, c)
    D_Z2, D_S = dev(a, z2, c), dev(a, z, oc)
    across = (1 - xh) * 4 + y
    dp_peers = [at_dp(y_of(dy)) for dy in (1, 2, 3)] + [at_dp(across)]

    barrier = pltpu.get_barrier_semaphore()

    @pl.loop(1, N_G)
    def _(r):
        pl.semaphore_signal(barrier, inc=1, device_id=peer(r)[1], device_id_type=MESH)

    for device in dp_peers:
        pl.semaphore_signal(barrier, inc=1, device_id=device, device_id_type=MESH)

    pairs = (
        (tok_hbm, tok.at[me]), (gain_a_hbm, gain_a), (seg_hbm, seg), (gain_f_hbm.at[me], gain_f),
        (wq_hbm, wq), (wk_hbm, wk), (wv_hbm, wv), (wo_hbm, wo), (wu_hbm, wu), (wd_hbm, wd),
    )
    loads = [pltpu.make_async_copy(h, v, w_sem.at[n]) for n, (h, v) in enumerate(pairs)]
    for load in loads:
        load.start()
    loads[0].wait()
    for h in range(2):
        own_a[h] = partial_stats(tok[me, h])
    stats_a[0] = own_a[...]
    pl.semaphore_wait(barrier, N_G - 1 + len(dp_peers))

    def stat_a(r):
        i, device = peer(r)
        return remote(own_a, stats_a.at[r], sa_send.at[0], sa_recv.at[0], device)

    def stat_f(h, r):
        i, device = peer(r)
        return remote(own_f.at[h], stats_f.at[h, r], sf_send.at[h], sf_recv.at[h], device)

    def all_of(ref, send_sem, recv_sem):
        return remote(ref, ref, send_sem, recv_sem, D_X)

    others_a = all_of(stats_a.at[pl.ds(1, N_G - 1)], sa_send.at[0], sa_recv.at[0])
    others_f = [all_of(stats_f.at[h, pl.ds(1, N_G - 1)], sf_send.at[h], sf_recv.at[h]) for h in range(2)]

    def norm_from(total, h):
        mean = total[0:1] / 8192.0
        second = total[1:2] / 8192.0
        inverse = lax.rsqrt(second - mean * mean + 1e-05)
        mu[h] = rows_to_columns(mean, WIDE)
        scale[h] = rows_to_columns(inverse, WIDE)

    def ag(s, h, device):
        remote(tok.at[s, h], tok.at[s, h], ag_send.at[0], ag_recv.at[s, h], device).start()

    def arrived(s, h):
        remote(tok.at[s, h], tok.at[s, h], ag_send.at[0], ag_recv.at[s, h], D_X).wait_recv()

    s_own, s_x, s_zp, s_zm = slot(a, z, c), slot(oa, z, c), slot(a, zp, c), slot(a, zm, c)
    s_z2, s_xzp, s_xzm, s_xz2 = slot(a, z2, c), slot(oa, zp, c), slot(oa, zm, c), slot(oa, z2, c)

    def other(s):
        return s + oc - c

    def project(s, h):
        x = (tok[s, h].astype(F32) - mu[h]) * scale[h] * gain_a[s]
        x = x.astype(BF16)
        at = pl.ds(pl.multiple_of(s * WIDE, WIDE), WIDE)
        for n, w in enumerate((wq, wk, wv)):
            acc[h, :, n * 256 : (n + 1) * 256] += jnp.dot(x, w[at, :], preferred_element_type=F32)

    def t_x(h):
        ag(s_own, h, D_X)

    def t_zz(h):
        ag(s_own, h, D_ZP)
        ag(s_own, h, D_ZM)

    def t_s(h):
        ag(s_own, h, D_S)

    def t_z2(h):
        ag(s_own, h, D_Z2)

    def t_fx(h):
        arrived(s_x, h)
        ag(s_x, h, D_ZP)
        ag(s_x, h, D_ZM)
        ag(s_x, h, D_S)

    def t_fz(h):
        for s in (s_zp, s_zm):
            arrived(s, h)
            ag(s, h, D_S)

    def t_f2(h):
        arrived(s_z2, h)
        ag(s_z2, h, D_X)
        ag(s_z2, h, D_S)

    def t_f3(h):
        for s in (s_xzp, s_xzm):
            arrived(s, h)
            ag(s, h, D_S)

    def t_f4(h):
        arrived(s_xz2, h)
        ag(s_xz2, h, D_S)

    def t_stat(h):
        @pl.loop(1, N_G)
        def _(r):
            stat_a(r).start()

    def t_norm(h):
        if h == 0:

            others_a.wait_recv()
            for n in range(2):
                norm_from(jnp.sum(stats_a[:, n], axis=0), n)
            acc[...] = jnp.zeros_like(acc)
            for n in (1, 2, 3, 4, 5, 6):
                loads[n].wait()

    def t_p0(h):
        project(s_own, h)
        arrived(other(s_own), h)
        project(other(s_own), h)

    def t_px(h):
        project(s_x, h)

    def t_pz(h):
        project(s_zp, h)
        project(s_zm, h)

    def t_p2(h):
        project(s_z2, h)

    def t_p3(h):
        project(s_xzp, h)
        project(s_xzm, h)

    def t_p4(h):
        project(s_xz2, h)

    def others(h, *slots):
        for s in slots:
            arrived(other(s), h)
            project(other(s), h)

    def t_qx(h):
        others(h, s_x)

    def t_qz(h):
        others(h, s_zp, s_zm)

    def t_q2(h):
        others(h, s_z2)

    def t_q3(h):
        others(h, s_xzp, s_xzm)

    def t_q4(h):
        others(h, s_xz2)

    def t_att(h):
        keys = (h + 1) * HALF
        seg_row = seg[...].astype(F32)
        seg_col = rows_to_columns(seg_row[:, h * HALF : (h + 1) * HALF], keys)
        at_q = lax.broadcasted_iota(jnp.int32, (HALF, keys), 0) + h * HALF
        at_k = lax.broadcasted_iota(jnp.int32, (HALF, keys), 1)
        keep = jnp.logical_and(at_q >= at_k, seg_col == seg_row[:, :keys])
        for head in range(2):

            def part_of(n, halves):
                cols = slice(n * 256 + head * HD, n * 256 + (head + 1) * HD)
                return jnp.concatenate([acc[i, :, cols].astype(BF16) for i in halves], axis=0)

            q, k, v = part_of(0, (h,)), part_of(1, range(h + 1)), part_of(2, range(h + 1))
            scores = lax.dot_general(q, k, (((1,), (1,)), ((), ())), preferred_element_type=F32)
            scores = jnp.where(keep, scores * HD ** (-0.5), -1e30)
            expo = jnp.exp(scores - jnp.max(scores, axis=-1, keepdims=True))
            probs = (expo / jnp.sum(expo, axis=-1, keepdims=True)).astype(BF16)
            context = jnp.dot(probs, v, preferred_element_type=F32)
            ctx[h, :, head * HD : (head + 1) * HD] = context.astype(BF16)

    order = ((oa, z2), (oa, zp), (oa, zm), (a, zp), (a, zm), (a, z2), (oa, z), (a, z))

    def term(s, h):
        at = pl.ds(pl.multiple_of(s * WIDE, WIDE), WIDE)
        return jnp.dot(ctx[h], wo[:, at], preferred_element_type=F32)

    def sib_copy(n, h):
        return remote(part.at[oc, n, h], sib.at[n, h], sib_send.at[0], sib_recv.at[n, h], D_S)

    def to_core(n, h):
        a_, z_ = order[n]
        part[oc, n, h] = term(slot(a_, z_, oc), h).astype(BF16)
        sib_copy(n, h).start()

    def t_opa(h):
        if h == 0:
            loads[7].wait()
        for n in range(AHEAD):
            to_core(n, h)

    red_to = (D_X, D_ZP, D_ZM, D_ZP, D_ZM, D_Z2, D_X)

    def red_copy(n, h):
        return remote(part.at[c, n, h], red.at[n, h], red_send.at[0], red_recv.at[n, h], red_to[n])

    def t_opb(h):
        for n, (a_, z_) in enumerate(order):
            if n + AHEAD < len(order):
                to_core(n + AHEAD, h)
            mine = term(slot(a_, z_, c), h)
            sib_copy(n, h).wait_recv()
            part[c, n, h] = (mine + sib[n, h].astype(F32)).astype(BF16)
            if n < 5:
                red_copy(n, h).start()

    def add_landed(n, h, *landings):
        total = part[c, n, h].astype(F32)
        for i in landings:
            red_copy(i, h).wait_recv()
            total += red[i, h].astype(F32)
        return total

    def t_r1(h):
        part[c, 5, h] = add_landed(5, h, 0).astype(BF16)
        red_copy(5, h).start()

    def t_r1b(h):
        part[c, 6, h] = add_landed(6, h, 1, 2).astype(BF16)
        red_copy(6, h).start()

    def t_r3(h):
        total = tok[me, h].astype(F32) + add_landed(7, h, 3, 4, 6, 5)
        resid[h] = total.astype(BF16)
        own_f[h] = partial_stats(resid[h])
        stats_f[h, 0] = own_f[h]

        @pl.loop(1, N_G)
        def _(r):
            stat_f(h, r).start()

    def nb_copy(h, s, device):
        return remote(nb.at[h, s], nb.at[h, s], nb_send.at[h], nb_recv.at[h, s], device)

    def nb_sends(h):
        to = (across, y_of(1), y_of(3), y_of(2))
        return [nb_copy(h, d, at_dp(d_)) for d_ in to]

    def nb_forwards(h):
        return [nb_copy(h, across, at_dp(y_of(dy))) for dy in (1, 3, 2)]

    def nb_arrived(h, s):
        nb_copy(h, s, at_dp(across)).wait_recv()

    def t_nb(h):
        others_f[h].wait_recv()
        norm_from(jnp.sum(stats_f[h], axis=0), h)
        normed = (resid[h].astype(F32) - mu[h]) * scale[h] * gain_f[...]
        nb[h, d] = normed.astype(BF16)
        for copy in nb_sends(h):
            copy.start()

    def half_of(k):
        return pick(k, [h for h, r in CHUNKS])

    def replica_of(k):
        return pick(k, [r for h, r in CHUNKS])

    def block(k, a_, z_):
        return up.at[k % RING, c, a_ * 4 + z_]

    def act_block(k, a_, z_):
        return act.at[k, c, a_ * 4 + z_]

    def copy_of(kind, k):
        at = land.at[k]
        src, dst, device = {
            SB: lambda: (up.at[k % RING, oc], sb.at[k], D_S),
            RX1: lambda: (block(k, oa, z2), at.at[L_RX1], D_X),
            RZP: lambda: (block(k, oa, zp), at.at[L_RZP], D_ZP),
            RZM: lambda: (block(k, oa, zm), at.at[L_RZM], D_ZM),
            FX: lambda: (block(k, oa, z), at.at[L_FX], D_X),
            FZP1: lambda: (block(k, a, zp).at[1], at.at[L_FZP, 1], D_ZP),
            FZM0: lambda: (block(k, a, zm).at[0], at.at[L_FZM, 0], D_ZM),
            H0: lambda: (block(k, a, z2).at[0], at.at[L_H, 0], D_ZP),
            H1: lambda: (block(k, a, z2).at[1], at.at[L_H, 1], D_ZM),
            FZP0: lambda: (block(k, a, zp).at[0], at.at[L_FZP, 0], D_ZP),
            FZM1: lambda: (block(k, a, zm).at[1], at.at[L_FZM, 1], D_ZM),
            FZP: lambda: (block(k, a, zp), at.at[L_FZP], D_ZP),
            FZM: lambda: (block(k, a, zm), at.at[L_FZM], D_ZM),
            FZ2: lambda: (block(k, a, z2), at.at[L_H], D_Z2),
            AX: lambda: (act_block(k, a, z),) * 2 + (D_X,),
            AZP: lambda: (act_block(k, a, z),) * 2 + (D_ZP,),
            AZM: lambda: (act_block(k, a, z),) * 2 + (D_ZM,),
            AZ2: lambda: (act_block(k, a, z),) * 2 + (D_Z2,),
            XZP: lambda: (act_block(k, oa, z),) * 2 + (D_ZP,),
            XZM: lambda: (act_block(k, oa, z),) * 2 + (D_ZM,),
            XZ2: lambda: (act_block(k, a, z2),) * 2 + (D_X,),
            ZH0: lambda: (act_block(k, a, zm).at[0],) * 2 + (D_ZP,),
            ZH1: lambda: (act_block(k, a, zp).at[1],) * 2 + (D_ZM,),
            AS: lambda: (act.at[k, c],) * 2 + (D_S,),
        }[kind]()
        sent = sum_send.at[k % RING] if kind < AX else act_send.at[0]
        return remote(src, dst, sent, recv.at[k % RING, GROUP_OF[kind]], device)

    def got(k, kind, ref):
        all_of(ref, act_send.at[0], recv.at[k % RING, GROUP_OF[kind]]).wait_recv()

    def give(k, *kinds):
        for kind in kinds:
            copy_of(kind, k).start()

    def either(condition, yes, no):
        pl.when(condition)(yes)
        pl.when(jnp.logical_not(condition))(no)

    def sums_sent(k):
        i = k % RING
        all_of(act.at[pl.ds(0, BLOCKS), 0, 0], sum_send.at[i], recv.at[0, 0]).wait_send()

    def sums_direct(k):
        return jnp.logical_and(k >= DIRECT_SUM[0], k < DIRECT_SUM[1])

    def up_product(k):
        h, r = half_of(k), replica_of(k)
        s = ((xh + r // 4) % 2) * 4 + (y + r % 4) % 4
        for n in range(2):

            @pl.when(k == FORWARD_AT[n])
            def _():
                nb_arrived(n, across)
                for copy in nb_forwards(n):
                    copy.start()

        @pl.when(pick(k, [int(r_ not in (0, 4)) for _, r_ in CHUNKS]) == 1)
        def _():
            nb_arrived(h, s)

        @pl.when(k >= RING)
        def _():
            sums_sent(k - RING)

        x = nb[h, s]
        for n in range(4):
            r_ = jnp.dot(x, wu[:, n * 512 : (n + 1) * 512], preferred_element_type=F32)
            up[k % RING, n // 2, :, n % 2] = r_.astype(BF16).reshape(8, 16, 512)
        give(k, SB)

    def pair_sum(k):
        got(k, SB, sb.at[k])
        i = k % RING
        up[i, c] = (up[i, c].astype(F32) + sb[k].astype(F32)).astype(BF16)
        give(k, RX1, RZP, RZM)
        either(sums_direct(k), lambda: give(k, FZP, FZM), lambda: give(k, FZP1, FZM0))

    def second_sum(k):
        i = k % RING
        got(k, RX1, land.at[k, L_RX1])
        b = a * 4 + z2
        up[i, c, b] = (up[i, c, b].astype(F32) + land[k, L_RX1].astype(F32)).astype(BF16)
        either(sums_direct(k), lambda: give(k, FZ2), lambda: give(k, H0, H1))
        got(k, RZP, land.at[k, pl.ds(L_RZP, 2)])
        b = oa * 4 + z
        both = land[k, L_RZP].astype(F32) + land[k, L_RZM].astype(F32)
        up[i, c, b] = (up[i, c, b].astype(F32) + both).astype(BF16)
        give(k, FX)

    def third_sum(k):
        i = k % RING

        @pl.when(jnp.logical_not(sums_direct(k)))
        def _():
            for kind, then, z_, half in ((H0, FZP0, zp, 0), (H1, FZM1, zm, 1)):
                got(k, kind, land.at[k, L_H, half])
                b = a * 4 + z_
                both = up[i, c, b, half].astype(F32) + land[k, L_H, half].astype(F32)
                up[i, c, b, half] = both.astype(BF16)
                give(k, then)

    def activate(k):
        i, b = k % RING, a * 4 + z

        def finish(pre, *landings):
            for n in landings:
                pre += land[k, n].astype(F32)
            inner = 0.7978845608028654 * (pre + 0.044715 * (pre * pre * pre))
            act[k, c, b] = (0.5 * pre * (1.0 + jnp.tanh(inner))).astype(BF16)

        def from_four():
            got(k, FX, land.at[k, pl.ds(L_FX, 4)])
            finish(up[i, c, b].astype(F32), L_FZP, L_FZM, L_FX, L_H)

        def from_three():
            got(k, FX, land.at[k, pl.ds(L_FX, 3)])
            finish(up[i, c, b].astype(F32), L_FZP, L_FZM, L_FX)

        either(sums_direct(k), from_four, from_three)

        @pl.when(k >= DIRECT_GATHER)
        def _():
            give(k, AZ2)

        give(k, AX, AZP, AZM)

    def spread(k):
        got(k, AX, act_block(k, oa, z))
        give(k, XZP, XZM)

        def direct():
            got(k, AZ2, act_block(k, a, z2))
            give(k, XZ2)

        def halves():
            got(k, AZP, act_block(k, a, zm))
            give(k, ZH0)
            got(k, AZM, act_block(k, a, zp))
            give(k, ZH1)

        either(k >= DIRECT_GATHER, direct, halves)

    def spread_across(k):
        def halves():
            got(k, ZH0, act_block(k, a, z2))
            give(k, XZ2)

        def direct():
            got(k, AZP, act_block(k, a, zm))
            got(k, AZM, act_block(k, a, zp))

        either(k >= DIRECT_GATHER, direct, halves)

    def down_half(k, c_):
        r = jnp.zeros((HALF, WIDE), F32)
        for q in range(2):
            x = act[k, c_, :, q].reshape(HALF, 512)
            r += jnp.dot(x, wd[c_ * 2 + q], preferred_element_type=F32)
        return r

    def to_sibling(k):
        got(k, XZP, act.at[k, c, pl.ds(0, 3)])
        give(k, AS)
        part_down[...] = down_half(k, c)

    def dp_copy(k):
        r = replica_of(k)
        x_ = (xh + pick(k, [int(r_ == 4) for _, r_ in CHUNKS])) % 2
        to = at_dp(x_ * 4 + (y + r % 4) % 4)
        return remote(down.at[k], fin.at[half_of(k), r], dp_send.at[0], dp_recv.at[half_of(k), r], to)

    def fin_arrived(h, r):
        remote(down.at[0], fin.at[h, r], dp_send.at[0], dp_recv.at[h, r], at_dp(across)).wait_recv()

    def is_sent(k):
        return pick(k, [int(r_ != 0) for _, r_ in CHUNKS]) == 1

    def down_product(k):
        got(k, AS, act.at[k, oc])
        down[k] = (part_down[...] + down_half(k, oc)).astype(BF16)
        for h in range(2):

            @pl.when(k == CHUNK_OF[h, 4])
            def _():
                total = down[k].astype(F32)
                for r in (5, 6, 7):
                    fin_arrived(h, r)
                    total += fin[h, r].astype(F32)
                down[k] = total.astype(BF16)

        @pl.when(is_sent(k))
        def _():
            dp_copy(k).start()

    tasks = {name[2:]: f for name, f in locals().items() if name.startswith("t_")}
    for name, h in (
        ("z2", 0), ("x", 0), ("stat", 0), ("s", 0), ("zz", 0), ("x", 1), ("fx", 0), ("fz", 0), ("f2", 0), ("zz", 1),
        ("norm", 0), ("p0", 0), ("pz", 0), ("fx", 1), ("px", 1), ("f3", 0), ("p2", 0), ("qz", 0), ("q2", 0),
        ("p3", 0), ("px", 0), ("qx", 1), ("f4", 0), ("p4", 0), ("q3", 0), ("z2", 1), ("qx", 0), ("fz", 1),
        ("q4", 0), ("att", 0), ("opa", 0), ("s", 1), ("opb", 0), ("p0", 1), ("f2", 1), ("r1b", 0), ("r1", 0),
        ("qz", 1), ("f3", 1), ("pz", 1), ("f4", 1), ("p3", 1), ("q2", 1), ("q3", 1), ("p2", 1), ("p4", 1),
        ("q4", 1), ("att", 1), ("r3", 0), ("opa", 1), ("opb", 1), ("nb", 0),
    ):
        tasks[name](h)
    loads[8].wait()
    loads[9].wait()
    up_product(0)
    t_r1b(1)
    t_r1(1)

    @pl.loop(0, N_K + 7)
    def _(step):
        pl.when(step == 2)(lambda: t_r3(1))
        pl.when(step == 4)(lambda: t_nb(1))
        for f, lag in (
            (pair_sum, 0), (up_product, -1), (second_sum, 1), (third_sum, 2), (activate, 3),
            (down_product, 7), (to_sibling, 6), (spread, 4), (spread_across, 5),
        ):
            k = step - lag
            pl.when(jnp.logical_and(k >= 0, k < N_K))(lambda f=f, k=k: f(k))

    for h in range(2):
        total = resid[h].astype(F32) + down[CHUNK_OF[h, 0]].astype(F32)
        for r in (1, 2, 3, 4):
            fin_arrived(h, r)
            total += fin[h, r].astype(F32)
        o_ref[h] = total.astype(BF16)

    others_a.wait_send()
    for h in range(2):
        others_f[h].wait_send()
        all_of(nb.at[h, pl.ds(0, 7)], nb_send.at[h], nb_recv.at[0, 0]).wait_send()
    all_of(tok.at[pl.ds(0, 15)], ag_send.at[0], ag_recv.at[0, 0]).wait_send()
    all_of(part.at[oc], sib_send.at[0], sib_recv.at[0, 0]).wait_send()
    all_of(part.at[c, pl.ds(0, 7)], red_send.at[0], red_recv.at[0, 0]).wait_send()
    all_of(down.at[pl.ds(0, 14)], dp_send.at[0], dp_recv.at[0, 0]).wait_send()
    all_of(act.at[pl.ds(0, BLOCKS)], act_send.at[0], recv.at[0, 0]).wait_send()

    @pl.loop(N_K - RING, N_K)
    def _(k):
        sums_sent(k)


def per_device(
    tokens, segment_ids, gain_attn, w_query, w_key, w_value, w_output, gain_ffn, w_up, w_down
):
    rows, share = tokens.shape
    vmem, hbm = pl.BlockSpec(memory_space=pltpu.VMEM), pl.BlockSpec(memory_space=pl.ANY)
    half = (HALF, share)
    dma = pltpu.SemaphoreType.DMA

    def b(*shape):
        return pltpu.VMEM(shape, BF16)

    def f(*shape):
        return pltpu.VMEM(shape, F32)

    out = pl.pallas_call(
        kernel,
        out_shape=jax.ShapeDtypeStruct((2, *half), BF16),
        in_specs=[hbm] * 10,
        out_specs=vmem,
        scratch_shapes=[
            pltpu.VMEM(segment_ids.shape, jnp.int32), f(N_G, 1, share), f(1, share),
            b(*w_query.shape), b(*w_query.shape), b(*w_query.shape), b(*w_output.shape),
            b(*w_up.shape), b(4, 512, share),
            b(N_G, 2, *half), f(2, HALF, 768), b(2, HALF, 256), b(2, 8, 2, *half), b(8, 2, *half),
            b(7, 2, *half), f(2, 8, HALF), f(2, 8, HALF), f(N_G, 2, 8, HALF), f(2, N_G, 8, HALF),
            f(2, *half), f(2, *half), b(2, *half),
            b(2, N_DP, *half), b(RING, 2, 8, 2, 16, 512), b(N_K, 8, 2, 16, 512), b(N_K, 7, 2, 16, 512),
            b(N_K, 2, 8, 2, 16, 512), f(*half), b(N_K, *half), b(2, N_DP, *half),
            dma((10,)), dma((1,)), dma((N_G, 2)), dma((1,)), dma((8, 2)), dma((1,)), dma((7, 2)),
            dma((1,)), dma((1,)), dma((2,)), dma((2,)),
            dma((RING,)), dma((1,)), dma((RING, len(GROUPS))), dma((2,)), dma((2, N_DP)), dma((1,)), dma((2, N_DP)),
        ],
        compiler_params=pltpu.CompilerParams(
            collective_id=0, has_side_effects=True, vmem_limit_bytes=62 << 20
        ),
        name="layer",
    )(
        tokens.reshape(2, *half), segment_ids, gain_attn.reshape(N_G, 1, share),
        gain_ffn.reshape(N_G, 1, share), w_query, w_key, w_value, w_output, w_up,
        w_down.reshape(4, 512, share),
    )
    return out.reshape(rows, share)


def solution(mesh):
    return jax.shard_map(
        per_device,
        mesh=mesh,
        in_specs=(
            P("dp", ("section", "tensor")),
            P("dp", None),
            P(),
            P(None, ("section", "tensor")),
            P(None, ("section", "tensor")),
            P(None, ("section", "tensor")),
            P(("section", "tensor"), None),
            P(),
            P(("section", "tensor"), "dp"),
            P("dp", ("section", "tensor")),
        ),
        out_specs=P("dp", ("section", "tensor")),
        check_vma=False,
    )
```
